768 devices in a mesh: dp: 96 (over z, x, core), group: 8 (over y).
Axes of the slice: x: 4, y: 8, z: 12, core: 2. Of those that a mesh axis runs over, the one named last changes fastest.
Arguments:
- partials: bfloat16 [96, 2304, 2048], P('dp', None, 'group')
- momentum: float32 [2304, 2048], P('dp', 'group'), may hold values from -6 to 6
Outputs:
- update: float32 [2304, 2048], P('dp', 'group')
- new_momentum: float32 [2304, 2048], P('dp', 'group')
The draws below stay inside these ranges and needn't reach their ends.
All inputs are finite; a program needn't handle non-finite values.
Results may differ from the reference program's by a relative error of at most 0.0003.
Values sent between devices are 32-bit elements; how exact they have to be, the bound alone decides.
No kernel may reach another device: no remote copies, remote signals or barrier semaphores. Data moves between devices by JAX's collectives and lax.ppermute only.
A program may use at most 32 MiB of HBM per device.

```python
import math
import jax
import jax.numpy as jnp
from jax import lax

D = 2048
KV_ROWS = 576
MATS = 4
ITERS = 2
N_DP = 96


def draw_partials(key, part):
    key = jax.random.fold_in(key, 11)
    key_base, key_col, key_row = jax.random.split(key, 3)
    base = jax.random.normal(key_base, (N_DP, MATS, KV_ROWS, D), jnp.float32)
    col_span = 10.0
    col_scale = jnp.exp(jax.random.uniform(key_col, (1, MATS, 1, D), jnp.float32) * jnp.log(col_span))
    row_scale = jnp.exp(jax.random.uniform(key_row, (1, MATS, KV_ROWS, 1), jnp.float32) * jnp.log(10.0))
    replica = 1.0 + 2.0 * jnp.arange(N_DP, dtype=jnp.float32) / max(N_DP - 1, 1)
    values = base * col_scale * row_scale * replica.reshape(N_DP, 1, 1, 1) * 0.005
    values = jnp.transpose(values, (0, 2, 1, 3))
    return values.reshape(N_DP, MATS * KV_ROWS, D).astype(jnp.bfloat16)


def level_of(stream_key, shape, shards, least, high):
    loudness = 1.0
    for axis_at, blocks in shards:
        heights = jax.random.uniform(jax.random.fold_in(jax.random.fold_in(stream_key, 6), axis_at), (blocks,), jnp.float32, least / len(shards), high / len(shards))
        loudness = loudness * jnp.repeat(jnp.exp(heights), shape[axis_at] // blocks).reshape((-1,) + (1,) * (len(shape) - 1 - axis_at))
    return loudness


def gaussian(own_key, extent, width, bound, cuts=(), kind=jnp.bfloat16):
    loudness = level_of(own_key, extent, cuts, -0.22, 0.18) if cuts else 1.0
    values = jax.random.normal(own_key, extent, jnp.float32) * width * loudness
    return jnp.minimum(jnp.maximum(values, -bound), bound).astype(kind)


def setup_inputs(seed: int = 0) -> dict:
    keys = jax.random.split(jax.random.key(seed), 3)
    return {
        "partials": draw_partials(jax.random.fold_in(keys[2], 71), 0),
        "momentum": gaussian(keys[1], (MATS * KV_ROWS, D), 1.0, 6.0, ((0, 96), (1, 8)), jnp.float32),
    }


coef_a = 3.4445
coef_b = -4.775
coef_c = 2.0315

def orthogonalize(matrices):
    frob_norm = jnp.sqrt(lax.optimization_barrier(jnp.sum(matrices * matrices, axis=(1, 2), keepdims=True)))
    ortho = matrices / (frob_norm + 1e-07)
    for sweep in range(ITERS):
        gram_matrix = jnp.einsum('mij,mkj->mik', ortho, ortho, precision=lax.Precision.HIGHEST)
        polynomial = coef_b * gram_matrix + coef_c * jnp.einsum('mij,mjk->mik', gram_matrix, gram_matrix, precision=lax.Precision.HIGHEST)
        ortho = coef_a * ortho + jnp.einsum('mij,mjk->mik', polynomial, ortho, precision=lax.Precision.HIGHEST)
    return ortho

def reference(partials, momentum):

    def accumulate(total, piece):
        return (total + piece.astype(jnp.float32), None)
    start_total = jnp.zeros(partials.shape[1:], jnp.float32)
    gradient, _ = lax.scan(accumulate, start_total, partials)
    new_momentum = 0.95 * momentum + gradient
    blended = gradient + 0.95 * new_momentum
    matrices = jnp.transpose(blended.reshape(KV_ROWS, MATS, D), (1, 0, 2))
    ortho = orthogonalize(matrices)
    scaled = 0.2 * math.sqrt(max(KV_ROWS, D)) * ortho
    update = jnp.transpose(scaled, (1, 0, 2)).reshape(MATS * KV_ROWS, D)
    return (update, new_momentum)
```

```python
import functools
import math

import jax
import jax.numpy as jnp
from jax import lax
from jax.experimental import pallas as pl
from jax.experimental.pallas import tpu as pltpu
from jax.sharding import Mesh
from jax.sharding import PartitionSpec as P

D = 2048
KV_ROWS = 576
MATS = 4
PADDED = 640
TILE = 128

coef_a = 3.4445
coef_b = -4.775
coef_c = 2.0315

GAIN = 1.95
KAPPA = 0.9025 / 1.95

PAIRS = [(i, j) for i in range(5) for j in range(i + 1)]
PAIRS.append(PAIRS[-1])

VMEM = pl.BlockSpec(memory_space=pltpu.VMEM)
SMEM = pl.BlockSpec(memory_space=pltpu.SMEM)
NT = (((1,), (1,)), ((), ()))
NN = (((1,), (0,)), ((), ()))


def split_kernel(place_ref, partial_ref, momentum_ref, keep_ref, send_ref, low, high):
    core, position = place_ref[0], place_ref[1]
    low[...] = partial_ref[:, :TILE].astype(jnp.float32)
    high[...] = partial_ref[:, TILE:].astype(jnp.float32)
    own = pl.ds(pl.multiple_of(position * 24, 8), 24)
    low[own, :] += KAPPA * momentum_ref[:, :TILE]
    high[own, :] += KAPPA * momentum_ref[:, TILE:]

    def put(mine, other):
        for m in range(MATS):
            rows = pl.ds(m, KV_ROWS, stride=MATS)
            keep_ref[m] = mine[rows, :]
            send_ref[m] = other[rows, :]

    @pl.when(core == 0)
    def _():
        put(low, high)

    @pl.when(core == 1)
    def _():
        put(high, low)


def split(place, partial, momentum):
    half = jax.ShapeDtypeStruct((MATS, KV_ROWS, TILE), jnp.float32)
    return pl.pallas_call(
        split_kernel,
        out_shape=(half, half),
        in_specs=[SMEM, VMEM, VMEM],
        out_specs=(VMEM, VMEM),
        scratch_shapes=[pltpu.VMEM((MATS * KV_ROWS, TILE), jnp.float32)] * 2,
        compiler_params=pltpu.CompilerParams(vmem_limit_bytes=24 << 20),
    )(place, partial, momentum)


def gram_kernel(place_ref, halves_ref, out_ref, rows):
    core = place_ref[0]
    rows[:KV_ROWS, :TILE] = halves_ref[0]
    rows[:KV_ROWS, TILE:] = halves_ref[1]
    rows[KV_ROWS:, :] = jnp.zeros((PADDED - KV_ROWS, 2 * TILE), jnp.float32)

    def put(pairs):
        for at, (i, j) in enumerate(pairs):
            out_ref[at] = lax.dot_general(
                rows[i * TILE : (i + 1) * TILE, :],
                rows[j * TILE : (j + 1) * TILE, :],
                NT,
                precision=lax.Precision.HIGHEST,
                preferred_element_type=jnp.float32,
            )

    @pl.when(core == 0)
    def _():
        put(PAIRS[:8])

    @pl.when(core == 1)
    def _():
        put(PAIRS[8:])


def gram(place, halves):
    return pl.pallas_call(
        gram_kernel,
        out_shape=jax.ShapeDtypeStruct((8, TILE, TILE), jnp.float32),
        in_specs=[SMEM, VMEM],
        out_specs=VMEM,
        scratch_shapes=[pltpu.VMEM((PADDED, 2 * TILE), jnp.float32)],
        compiler_params=pltpu.CompilerParams(vmem_limit_bytes=24 << 20),
    )(place, halves)


def three(x):
    top = x.astype(jnp.bfloat16)
    rest = x - top.astype(jnp.float32)
    middle = rest.astype(jnp.bfloat16)
    bottom = (rest - middle.astype(jnp.float32)).astype(jnp.bfloat16)
    return top, middle, bottom


def times(x, right):
    n = x.shape[0]
    top, middle, bottom = three(x)
    dot = functools.partial(
        lax.dot_general, dimension_numbers=NN, preferred_element_type=jnp.float32
    )
    by_top = dot(jnp.concatenate([top, middle, bottom], 0), right[0][...])
    by_middle = dot(jnp.concatenate([top, middle], 0), right[1][...])
    by_bottom = dot(top, right[2][...])
    small = by_top[2 * n :] + by_middle[n:] + by_bottom
    return by_top[:n] + (by_top[n : 2 * n] + by_middle[:n] + small)


def chain_kernel(place_ref, blocks_ref, halves_ref, out_ref, g0, g1, g2, t0, t1, t2):
    core, z = place_ref[0], place_ref[2]
    row = lax.broadcasted_iota(jnp.int32, (TILE, TILE), 0)
    column = lax.broadcasted_iota(jnp.int32, (TILE, TILE), 1)
    diagonal = jnp.zeros((TILE, TILE), jnp.float32)
    for at, (i, j) in enumerate(PAIRS[:15]):
        if i == j:
            diagonal += jnp.where(row == column, blocks_ref[at], 0.0)
    squares = jnp.sum(jnp.sum(diagonal, axis=0, keepdims=True), axis=1, keepdims=True)
    scale = GAIN / (GAIN * jnp.sqrt(squares) + 1e-07)
    for at, (i, j) in enumerate(PAIRS[:15]):
        block = (blocks_ref[at] * scale) * scale
        here = (slice(i * TILE, (i + 1) * TILE), slice(j * TILE, (j + 1) * TILE))
        for ref, part in zip((g0, g1, g2), three(block)):
            ref[here] = part
        if i != j:
            for ref, part in zip((g0, g1, g2), three(block.T)):
                ref[here[1], here[0]] = part
    for half in range(2):
        for ref, part in zip((t0, t1, t2), three(halves_ref[half])):
            ref[:KV_ROWS, half * TILE : (half + 1) * TILE] = part
    for ref in (t0, t1, t2):
        ref[KV_ROWS:, :] = jnp.zeros((PADDED - KV_ROWS, 2 * TILE), jnp.bfloat16)
    g, t = (g0, g1, g2), (t0, t1, t2)

    r = lax.broadcasted_iota(jnp.int32, (32, PADDED), 0)
    k = lax.broadcasted_iota(jnp.int32, (32, PADDED), 1)
    wanted = 48 * z + 6 * core + 12 * (r >> 3) + (r & 7)
    pick = jnp.where(jnp.logical_and(k == wanted, (r & 7) < 6), 1.0, 0.0)

    def poly(x):
        once = times(x, g)
        return coef_a * x + coef_b * once + coef_c * times(once, g)

    first = poly(pick)
    second = times(poly(poly(first)), g)
    third = times(poly(poly(second)), g)
    rows = coef_a * first + coef_b * second + coef_c * third
    gain = (0.2 * math.sqrt(max(KV_ROWS, D))) * scale
    update = gain * times(rows, t)
    own = times(pick, t)
    for x in range(4):
        out_ref[x, :8, :] = update[8 * x : 8 * x + 8]
        out_ref[x, 8:, :] = own[8 * x : 8 * x + 8]


def chain(place, blocks, halves):
    return pl.pallas_call(
        chain_kernel,
        out_shape=jax.ShapeDtypeStruct((4, 16, 2 * TILE), jnp.float32),
        in_specs=[SMEM, VMEM, VMEM],
        out_specs=VMEM,
        scratch_shapes=[pltpu.VMEM((PADDED, PADDED), jnp.bfloat16)] * 3
        + [pltpu.VMEM((PADDED, 2 * TILE), jnp.bfloat16)] * 3,
        compiler_params=pltpu.CompilerParams(vmem_limit_bytes=24 << 20),
    )(place, blocks, halves)


def finish_kernel(got_ref, momentum_ref, update_ref, new_ref, update_half, sum_half):
    for half in range(2):
        columns = slice(half * TILE, (half + 1) * TILE)
        for m in range(MATS):
            rows = pl.ds(m, 6, stride=MATS)
            update_half[rows, :] = got_ref[m, 0:6, columns]
            sum_half[rows, :] = got_ref[m, 8:14, columns]
        momentum = momentum_ref[:, columns]
        update_ref[:, columns] = update_half[...]
        new_ref[:, columns] = 0.95 * momentum + (sum_half[...] - KAPPA * momentum)


def finish(got, momentum):
    shape = jax.ShapeDtypeStruct(momentum.shape, jnp.float32)
    return pl.pallas_call(
        finish_kernel,
        out_shape=(shape, shape),
        in_specs=[VMEM, VMEM],
        out_specs=(VMEM, VMEM),
        scratch_shapes=[pltpu.VMEM((24, TILE), jnp.float32)] * 2,
    )(got, momentum)


def exchange(x, axis):
    return lax.all_to_all(x, axis, split_axis=0, concat_axis=0, tiled=True)


def spread(x, axis):
    count = lax.axis_size(axis)
    return exchange(jnp.broadcast_to(x[None], (count, *x.shape)), axis)


def per_device(partials, momentum):
    z, x, c = lax.axis_index("z"), lax.axis_index("x"), lax.axis_index("c")
    place = jnp.stack([c, (z * 4 + x) * 2 + c, z]).astype(jnp.int32)
    keep, send = split(place, partials[0], momentum)
    got = lax.ppermute(send, "c", [(0, 1), (1, 0)])
    by_x = exchange(keep + got, "x")
    by_z = exchange(jnp.sum(by_x, axis=0).reshape(12, 48, TILE), "z")
    own = jnp.sum(by_z, axis=0)
    half = spread(own, "z").reshape(KV_ROWS, TILE)
    halves = lax.all_gather(half, "c", axis=0, tiled=False)
    terms = exchange(gram(place, halves), "y")
    block = jnp.sum(terms, axis=0)
    blocks = lax.all_gather(spread(block, "y"), "c", axis=0, tiled=True)
    done = chain(place, blocks, halves)
    return finish(exchange(done, "x"), momentum)


def solution(mesh):
    fine = Mesh(mesh.devices.reshape(12, 4, 2, 8), ("z", "x", "c", "y"))
    rows = ("z", "x", "c")
    return jax.shard_map(
        per_device,
        mesh=fine,
        in_specs=(P(rows, None, "y"), P(rows, "y")),
        out_specs=(P(rows, "y"), P(rows, "y")),
        check_vma=False,
    )
```

```python
import functools
import math

import jax
import jax.numpy as jnp
from jax import lax
from jax.experimental import pallas as pl
from jax.experimental.pallas import tpu as pltpu
from jax.sharding import Mesh
from jax.sharding import PartitionSpec as P

D = 2048
KV_ROWS = 576
MATS = 4
PADDED = 640
TILE = 128

coef_a = 3.4445
coef_b = -4.775
coef_c = 2.0315

GAIN = 1.95
KAPPA = 0.9025 / 1.95

BLOCK = 64

STRIPS = [((0, 0), (8, 8))]
STRIPS += [
    ((i, 2 * j), (i, 2 * j + 1))
    for i in range(1, 9)
    for j in range(i // 2 + 1)
    if (i, j) != (8, 4)
]
PAIRS = [(i, j) for i in range(5) for j in range(i + 1)]

VMEM = pl.BlockSpec(memory_space=pltpu.VMEM)
SMEM = pl.BlockSpec(memory_space=pltpu.SMEM)
NT = (((1,), (1,)), ((), ()))
NN = (((1,), (0,)), ((), ()))


def split_kernel(place_ref, partial_ref, momentum_ref, keep_ref, send_ref, low, high):
    core, position = place_ref[0], place_ref[1]
    low[...] = partial_ref[:, :TILE].astype(jnp.float32)
    high[...] = partial_ref[:, TILE:].astype(jnp.float32)
    own = pl.ds(pl.multiple_of(position * 24, 8), 24)
    low[own, :] += KAPPA * momentum_ref[:, :TILE]
    high[own, :] += KAPPA * momentum_ref[:, TILE:]

    def put(mine, other):
        for m in range(MATS):
            rows = pl.ds(m, KV_ROWS, stride=MATS)
            keep_ref[:, m] = mine[rows, :].reshape(12, 48, TILE)
            send_ref[:, m] = other[rows, :].reshape(12, 48, TILE)

    @pl.when(core == 0)
    def _():
        put(low, high)

    @pl.when(core == 1)
    def _():
        put(high, low)


def split(place, partial, momentum):
    half = jax.ShapeDtypeStruct((12, MATS, 48, TILE), jnp.float32)
    return pl.pallas_call(
        split_kernel,
        out_shape=(half, half),
        in_specs=[SMEM, VMEM, VMEM],
        out_specs=(VMEM, VMEM),
        scratch_shapes=[pltpu.VMEM((MATS * KV_ROWS, TILE), jnp.float32)] * 2,
        compiler_params=pltpu.CompilerParams(vmem_limit_bytes=24 << 20),
    )(place, partial, momentum)


def gram_kernel(table_ref, halves_ref, out_ref, rows):
    rows[:, :TILE] = halves_ref[0]
    rows[:, TILE:] = halves_ref[1]
    for side in range(2):
        left, right = (
            rows[pl.ds(pl.multiple_of(table_ref[2 * side + k] * BLOCK, BLOCK), BLOCK), :]
            for k in range(2)
        )
        out_ref[:, side * BLOCK : (side + 1) * BLOCK] = lax.dot_general(
            left,
            right,
            NT,
            precision=lax.Precision.HIGHEST,
            preferred_element_type=jnp.float32,
        )


def gram(strip, halves):
    table = jnp.asarray(STRIPS, jnp.int32).reshape(24, 4)
    return pl.pallas_call(
        gram_kernel,
        out_shape=jax.ShapeDtypeStruct((BLOCK, TILE), jnp.float32),
        in_specs=[SMEM, VMEM],
        out_specs=VMEM,
        scratch_shapes=[pltpu.VMEM((KV_ROWS, 2 * TILE), jnp.float32)],
        compiler_params=pltpu.CompilerParams(vmem_limit_bytes=24 << 20),
    )(lax.dynamic_index_in_dim(table, strip, 0, keepdims=False), halves)


def three(x):
    top = x.astype(jnp.bfloat16)
    rest = x - top.astype(jnp.float32)
    middle = rest.astype(jnp.bfloat16)
    bottom = (rest - middle.astype(jnp.float32)).astype(jnp.bfloat16)
    return top, middle, bottom


def times(x, right):
    n = x.shape[0]
    top, middle, bottom = three(x)
    dot = functools.partial(
        lax.dot_general, dimension_numbers=NN, preferred_element_type=jnp.float32
    )
    by_top = dot(jnp.concatenate([top, middle, bottom], 0), right[0][...])
    by_middle = dot(jnp.concatenate([top, middle], 0), right[1][...])
    by_bottom = dot(top, right[2][...])
    small = by_top[2 * n :] + by_middle[n:] + by_bottom
    return by_top[:n] + (by_top[n : 2 * n] + by_middle[:n] + small)


def triangle(strips_ref):
    zero = jnp.zeros((BLOCK, BLOCK), jnp.float32)
    strip = {}
    for at, ((i, j), other) in enumerate(STRIPS[1:], 1):
        strip[i, j // 2] = strips_ref[at]
    ends = strips_ref[0]
    strip[0, 0] = jnp.concatenate([ends[:, :BLOCK], strip[1, 0][:, :BLOCK].T], 1)
    strip[8, 4] = jnp.concatenate([ends[:, BLOCK:], zero], 1)
    blank = jnp.concatenate([zero, zero], 1)
    return {
        (i, j): jnp.concatenate([strip[2 * i, j], strip.get((2 * i + 1, j), blank)], 0)
        for i, j in PAIRS
    }


def chain_kernel(place_ref, strips_ref, halves_ref, out_ref, g0, g1, g2, t0, t1, t2):
    first_row = place_ref[2]
    blocks = triangle(strips_ref)
    row = lax.broadcasted_iota(jnp.int32, (TILE, TILE), 0)
    column = lax.broadcasted_iota(jnp.int32, (TILE, TILE), 1)
    diagonal = jnp.zeros((TILE, TILE), jnp.float32)
    for i in range(5):
        diagonal += jnp.where(row == column, blocks[i, i], 0.0)
    squares = jnp.sum(jnp.sum(diagonal, axis=0, keepdims=True), axis=1, keepdims=True)
    scale = GAIN / (GAIN * jnp.sqrt(squares) + 1e-07)
    for i, j in PAIRS:
        block = (blocks[i, j] * scale) * scale
        here = (slice(i * TILE, (i + 1) * TILE), slice(j * TILE, (j + 1) * TILE))
        for ref, part in zip((g0, g1, g2), three(block)):
            ref[here] = part
        if i != j:
            for ref, part in zip((g0, g1, g2), three(block.T)):
                ref[here[1], here[0]] = part
    for half in range(2):
        for ref, part in zip((t0, t1, t2), three(halves_ref[half])):
            ref[:KV_ROWS, half * TILE : (half + 1) * TILE] = part
    for ref in (t0, t1, t2):
        ref[KV_ROWS:, :] = jnp.zeros((PADDED - KV_ROWS, 2 * TILE), jnp.bfloat16)
    g, t = (g0, g1, g2), (t0, t1, t2)

    r = lax.broadcasted_iota(jnp.int32, (32, PADDED), 0)
    k = lax.broadcasted_iota(jnp.int32, (32, PADDED), 1)
    wanted = first_row + 144 * (r >> 3) + (r & 7)
    pick = jnp.where(jnp.logical_and(k == wanted, (r & 7) < 6), 1.0, 0.0)

    def poly(x):
        once = times(x, g)
        return coef_a * x + coef_b * once + coef_c * times(once, g)

    first = poly(pick)
    second = times(poly(poly(first)), g)
    third = times(poly(poly(second)), g)
    rows = coef_a * first + coef_b * second + coef_c * third
    gain = (0.2 * math.sqrt(max(KV_ROWS, D))) * scale
    update = gain * times(rows, t)
    own = times(pick, t)
    for x in range(4):
        out_ref[x, :8, :] = update[8 * x : 8 * x + 8]
        out_ref[x, 8:, :] = own[8 * x : 8 * x + 8]


def chain(place, strips, halves):
    return pl.pallas_call(
        chain_kernel,
        out_shape=jax.ShapeDtypeStruct((4, 16, 2 * TILE), jnp.float32),
        in_specs=[SMEM, VMEM, VMEM],
        out_specs=VMEM,
        scratch_shapes=[pltpu.VMEM((PADDED, PADDED), jnp.bfloat16)] * 3
        + [pltpu.VMEM((PADDED, 2 * TILE), jnp.bfloat16)] * 3,
        compiler_params=pltpu.CompilerParams(vmem_limit_bytes=24 << 20),
    )(place, strips, halves)


def finish_kernel(got_ref, momentum_ref, update_ref, new_ref, update_half, sum_half):
    for half in range(2):
        columns = slice(half * TILE, (half + 1) * TILE)
        for m in range(MATS):
            rows = pl.ds(m, 6, stride=MATS)
            update_half[rows, :] = got_ref[m, 0:6, columns]
            sum_half[rows, :] = got_ref[m, 8:14, columns]
        momentum = momentum_ref[:, columns]
        update_ref[:, columns] = update_half[...]
        new_ref[:, columns] = 0.95 * momentum + (sum_half[...] - KAPPA * momentum)


def finish(got, momentum):
    shape = jax.ShapeDtypeStruct(momentum.shape, jnp.float32)
    return pl.pallas_call(
        finish_kernel,
        out_shape=(shape, shape),
        in_specs=[VMEM, VMEM],
        out_specs=(VMEM, VMEM),
        scratch_shapes=[pltpu.VMEM((24, TILE), jnp.float32)] * 2,
    )(got, momentum)


def exchange(x, axis):
    return lax.all_to_all(x, axis, split_axis=0, concat_axis=0, tiled=True)


def spread(x, axis, count):
    return exchange(jnp.broadcast_to(x[None], (count, *x.shape)), axis)


def per_device(partials, momentum):
    w, v, x, c = (lax.axis_index(name) for name in ("w", "v", "x", "c"))
    z = 3 * w + v
    first_row = 48 * v + 12 * x + 6 * c
    place = jnp.stack([c, (z * 4 + x) * 2 + c, first_row]).astype(jnp.int32)
    keep, send = split(place, partials[0], momentum)
    got = lax.ppermute(send, "c", [(0, 1), (1, 0)])
    near = jnp.sum(exchange(keep + got, ("v", "x")), axis=0)
    own = jnp.sum(exchange(near, "w"), axis=0)
    half = spread(own, ("v", "x"), 12).reshape(KV_ROWS, TILE)
    halves = lax.all_gather(half, "c", axis=0, tiled=False)
    strip = jnp.sum(spread(gram(c * 12 + v * 4 + x, halves), "y", 8), axis=0)
    strips = lax.all_gather(spread(strip, ("v", "x"), 12), "c", axis=0, tiled=True)
    done = chain(place, strips, halves)
    return finish(exchange(done, "w"), momentum)


def solution(mesh):
    fine = Mesh(mesh.devices.reshape(4, 3, 4, 2, 8), ("w", "v", "x", "c", "y"))
    rows = ("w", "v", "x", "c")
    return jax.shard_map(
        per_device,
        mesh=fine,
        in_specs=(P(rows, None, "y"), P(rows, "y")),
        out_specs=(P(rows, "y"), P(rows, "y")),
        check_vma=False,
    )
```

```python
import functools
import math

import jax
import jax.numpy as jnp
import numpy as np
from jax import lax
from jax.experimental import pallas as pl
from jax.experimental.pallas import tpu as pltpu
from jax.sharding import Mesh
from jax.sharding import PartitionSpec as P

D = 2048
KV_ROWS = 576
MATS = 4
PADDED = 640
TILE = 128

coef_a = 3.4445
coef_b = -4.775
coef_c = 2.0315

GAIN = 1.95
KAPPA = 0.9025 / 1.95

BLOCK = 64

STRIPS = [((0, 0), (8, 8))]
STRIPS += [
    ((i, 2 * j), (i, 2 * j + 1))
    for i in range(1, 9)
    for j in range(i // 2 + 1)
    if (i, j) != (8, 4)
]
STARTS = [next(n for n, (a, _) in enumerate(STRIPS) if a[0] == i) for i in range(9)]
PAIRS = [(i, j) for i in range(5) for j in range(i + 1)]

VMEM = pl.BlockSpec(memory_space=pltpu.VMEM)
SMEM = pl.BlockSpec(memory_space=pltpu.SMEM)
NT = (((1,), (1,)), ((), ()))
NN = (((1,), (0,)), ((), ()))


def split_kernel(place_ref, partial_ref, momentum_ref, keep_ref, send_ref, low, high):
    core, position = place_ref[0], place_ref[1]
    low[...] = partial_ref[:, :TILE].astype(jnp.float32)
    high[...] = partial_ref[:, TILE:].astype(jnp.float32)
    own = pl.ds(pl.multiple_of(position * 24, 8), 24)
    low[own, :] += KAPPA * momentum_ref[:, :TILE]
    high[own, :] += KAPPA * momentum_ref[:, TILE:]

    def put(mine, other):
        for m in range(MATS):
            rows = pl.ds(m, KV_ROWS, stride=MATS)
            keep_ref[:, m] = mine[rows, :].reshape(12, 48, TILE)
            send_ref[:, m] = other[rows, :].reshape(12, 48, TILE)

    @pl.when(core == 0)
    def _():
        put(low, high)

    @pl.when(core == 1)
    def _():
        put(high, low)


def split(place, partial, momentum):
    half = jax.ShapeDtypeStruct((12, MATS, 48, TILE), jnp.float32)
    return pl.pallas_call(
        split_kernel,
        out_shape=(half, half),
        in_specs=[SMEM, VMEM, VMEM],
        out_specs=(VMEM, VMEM),
        scratch_shapes=[pltpu.VMEM((MATS * KV_ROWS, TILE), jnp.float32)] * 2,
        compiler_params=pltpu.CompilerParams(vmem_limit_bytes=24 << 20),
    )(place, partial, momentum)


def gram_kernel(place_ref, halves_ref, out_ref, rows):
    rows[:, :TILE] = halves_ref[0]
    rows[:, TILE:] = halves_ref[1]
    strip = place_ref[3]
    i, start = jnp.int32(0), jnp.int32(0)
    for begin, step in zip(STARTS[1:], np.diff(STARTS)):
        past = strip >= begin
        i += past.astype(jnp.int32)
        start += jnp.where(past, int(step), 0)
    j = 2 * (strip - start)
    ends = strip == 0
    sides = [(i, j), (jnp.where(ends, 8, i), jnp.where(ends, 8, j + 1))]
    for side, pair in enumerate(sides):
        left, right = (rows[pl.ds(pl.multiple_of(k * BLOCK, BLOCK), BLOCK), :] for k in pair)
        out_ref[:, side * BLOCK : (side + 1) * BLOCK] = lax.dot_general(
            left,
            right,
            NT,
            precision=lax.Precision.HIGHEST,
            preferred_element_type=jnp.float32,
        )


def gram(place, halves):
    return pl.pallas_call(
        gram_kernel,
        out_shape=jax.ShapeDtypeStruct((BLOCK, TILE), jnp.float32),
        in_specs=[SMEM, VMEM],
        out_specs=VMEM,
        scratch_shapes=[pltpu.VMEM((KV_ROWS, 2 * TILE), jnp.float32)],
        compiler_params=pltpu.CompilerParams(vmem_limit_bytes=24 << 20),
    )(place, halves)


def three(x):
    top = x.astype(jnp.bfloat16)
    rest = x - top.astype(jnp.float32)
    middle = rest.astype(jnp.bfloat16)
    bottom = (rest - middle.astype(jnp.float32)).astype(jnp.bfloat16)
    return top, middle, bottom


def times(x, right):
    n = x.shape[0]
    parts = three(x)
    total = 0.0
    for at, ref in reversed(list(enumerate(right))):
        product = lax.dot_general(
            jnp.concatenate(parts[: 3 - at], 0),
            ref[...],
            NN,
            preferred_element_type=jnp.float32,
        )
        for k in reversed(range(3 - at)):
            total = total + product[k * n : (k + 1) * n]
    return total


def triangle(strips_ref):
    zero = jnp.zeros((BLOCK, BLOCK), jnp.float32)
    strip = {}
    for at, ((i, j), other) in enumerate(STRIPS[1:], 1):
        strip[i, j // 2] = strips_ref[at]
    ends = strips_ref[0]
    strip[0, 0] = jnp.concatenate([ends[:, :BLOCK], strip[1, 0][:, :BLOCK].T], 1)
    strip[8, 4] = jnp.concatenate([ends[:, BLOCK:], zero], 1)
    blank = jnp.concatenate([zero, zero], 1)
    return {
        (i, j): jnp.concatenate([strip[2 * i, j], strip.get((2 * i + 1, j), blank)], 0)
        for i, j in PAIRS
    }


def chain_kernel(place_ref, strips_ref, halves_ref, out_ref, g0, g1, t0, t1, t2):
    first_row = place_ref[2]
    blocks = triangle(strips_ref)
    row = lax.broadcasted_iota(jnp.int32, (TILE, TILE), 0)
    column = lax.broadcasted_iota(jnp.int32, (TILE, TILE), 1)
    diagonal = jnp.zeros((TILE, TILE), jnp.float32)
    for i in range(5):
        diagonal += jnp.where(row == column, blocks[i, i], 0.0)
    squares = jnp.sum(jnp.sum(diagonal, axis=0, keepdims=True), axis=1, keepdims=True)
    scale = GAIN / (GAIN * jnp.sqrt(squares) + 1e-07)
    for i, j in PAIRS:
        block = (blocks[i, j] * scale) * scale
        here = (slice(i * TILE, (i + 1) * TILE), slice(j * TILE, (j + 1) * TILE))
        for ref, part in zip((g0, g1), three(block)):
            ref[here] = part
        if i != j:
            for ref, part in zip((g0, g1), three(block.T)):
                ref[here[1], here[0]] = part
    for half in range(2):
        for ref, part in zip((t0, t1, t2), three(halves_ref[half])):
            ref[:KV_ROWS, half * TILE : (half + 1) * TILE] = part
    for ref in (t0, t1, t2):
        ref[KV_ROWS:, :] = jnp.zeros((PADDED - KV_ROWS, 2 * TILE), jnp.bfloat16)
    g, t = (g0, g1), (t0, t1, t2)

    r = lax.broadcasted_iota(jnp.int32, (32, PADDED), 0)
    k = lax.broadcasted_iota(jnp.int32, (32, PADDED), 1)
    wanted = first_row + 144 * (r >> 3) + (r & 7)
    pick = jnp.where(jnp.logical_and(k == wanted, (r & 7) < 6), 1.0, 0.0)

    def poly(x):
        once = times(x, g)
        return coef_a * x + coef_b * once + coef_c * times(once, g)

    first = poly(pick)
    second = times(poly(poly(first)), g)
    third = times(poly(poly(second)), g)
    rows = coef_a * first + coef_b * second + coef_c * third
    gain = (0.2 * math.sqrt(max(KV_ROWS, D))) * scale
    update = gain * times(rows, t)
    own = times(pick, t)
    for x in range(4):
        out_ref[x, :8, :] = update[8 * x : 8 * x + 8]
        out_ref[x, 8:, :] = own[8 * x : 8 * x + 8]


def chain(place, strips, halves):
    return pl.pallas_call(
        chain_kernel,
        out_shape=jax.ShapeDtypeStruct((4, 16, 2 * TILE), jnp.float32),
        in_specs=[SMEM, VMEM, VMEM],
        out_specs=VMEM,
        scratch_shapes=[pltpu.VMEM((PADDED, PADDED), jnp.bfloat16)] * 2
        + [pltpu.VMEM((PADDED, 2 * TILE), jnp.bfloat16)] * 3,
        compiler_params=pltpu.CompilerParams(vmem_limit_bytes=24 << 20),
    )(place, strips, halves)


def finish_kernel(got_ref, momentum_ref, update_ref, new_ref, update_half, sum_half):
    for half in range(2):
        columns = slice(half * TILE, (half + 1) * TILE)
        for m in range(MATS):
            rows = pl.ds(m, 6, stride=MATS)
            update_half[rows, :] = got_ref[m, 0:6, columns]
            sum_half[rows, :] = got_ref[m, 8:14, columns]
        momentum = momentum_ref[:, columns]
        update_ref[:, columns] = update_half[...]
        new_ref[:, columns] = 0.95 * momentum + (sum_half[...] - KAPPA * momentum)


def finish(got, momentum):
    shape = jax.ShapeDtypeStruct(momentum.shape, jnp.float32)
    return pl.pallas_call(
        finish_kernel,
        out_shape=(shape, shape),
        in_specs=[VMEM, VMEM],
        out_specs=(VMEM, VMEM),
        scratch_shapes=[pltpu.VMEM((24, TILE), jnp.float32)] * 2,
    )(got, momentum)


def exchange(x, axis):
    return lax.all_to_all(x, axis, split_axis=0, concat_axis=0, tiled=True)


def spread(x, axis, count):
    return exchange(jnp.broadcast_to(x[None], (count, *x.shape)), axis)


def per_device(partials, momentum):
    w, v, x, c = (lax.axis_index(name) for name in ("w", "v", "x", "c"))
    z = 3 * w + v
    first_row = 48 * v + 12 * x + 6 * c
    strip = c * 12 + v * 4 + x
    place = jnp.stack([c, (z * 4 + x) * 2 + c, first_row, strip]).astype(jnp.int32)
    keep, send = split(place, partials[0], momentum)
    got = lax.ppermute(send, "c", [(0, 1), (1, 0)])
    near = jnp.sum(exchange(keep + got, ("v", "x")), axis=0)
    own = jnp.sum(exchange(near, "w"), axis=0)
    half = spread(own, ("v", "x"), 12).reshape(KV_ROWS, TILE)
    halves = lax.all_gather(half, "c", axis=0, tiled=False)
    mine = jnp.sum(spread(gram(place, halves), "y", 8), axis=0)
    strips = lax.all_gather(spread(mine, ("v", "x"), 12), "c", axis=0, tiled=True)
    done = chain(place, strips, halves)
    return finish(exchange(done, "w"), momentum)


def solution(mesh):
    fine = Mesh(mesh.devices.reshape(4, 3, 4, 2, 8), ("w", "v", "x", "c", "y"))
    rows = ("w", "v", "x", "c")
    return jax.shard_map(
        per_device,
        mesh=fine,
        in_specs=(P(rows, None, "y"), P(rows, "y")),
        out_specs=(P(rows, "y"), P(rows, "y")),
        check_vma=False,
    )
```

```python
import functools
import math

import jax
import jax.numpy as jnp
import numpy as np
from jax import lax
from jax.experimental import pallas as pl
from jax.experimental.pallas import tpu as pltpu
from jax.sharding import Mesh
from jax.sharding import PartitionSpec as P

D = 2048
KV_ROWS = 576
MATS = 4
PADDED = 640
TILE = 128

coef_a = 3.4445
coef_b = -4.775
coef_c = 2.0315

GAIN = 1.95
KAPPA = 0.9025 / 1.95

BLOCK = 64

STRIPS = [((0, 0), (8, 8))]
STRIPS += [
    ((i, 2 * j), (i, 2 * j + 1))
    for i in range(1, 9)
    for j in range(i // 2 + 1)
    if (i, j) != (8, 4)
]
STARTS = [next(n for n, (a, _) in enumerate(STRIPS) if a[0] == i) for i in range(9)]
PAIRS = [(i, j) for i in range(5) for j in range(i + 1)]

VMEM = pl.BlockSpec(memory_space=pltpu.VMEM)
SMEM = pl.BlockSpec(memory_space=pltpu.SMEM)
NT = (((1,), (1,)), ((), ()))
NN = (((1,), (0,)), ((), ()))


def split_kernel(place_ref, partial_ref, momentum_ref, *refs):
    keep_refs, send_refs, (low, high) = refs[:2], refs[2:4], refs[4:]
    core, position = place_ref[0], place_ref[1]
    low[...] = partial_ref[:, :TILE].astype(jnp.float32)
    high[...] = partial_ref[:, TILE:].astype(jnp.float32)
    own = pl.ds(pl.multiple_of(position * 24, 8), 24)
    low[own, :] += KAPPA * momentum_ref[:, :TILE]
    high[own, :] += KAPPA * momentum_ref[:, TILE:]

    def put(mine, other):
        for m in range(MATS):
            rows = pl.ds(m, KV_ROWS, stride=MATS)
            keep_refs[m // 2][:, m % 2] = mine[rows, :].reshape(12, 48, TILE)
            send_refs[m // 2][:, m % 2] = other[rows, :].reshape(12, 48, TILE)

    @pl.when(core == 0)
    def _():
        put(low, high)

    @pl.when(core == 1)
    def _():
        put(high, low)


def split(place, partial, momentum):
    part = jax.ShapeDtypeStruct((12, MATS // 2, 48, TILE), jnp.float32)
    return pl.pallas_call(
        split_kernel,
        out_shape=(part,) * 4,
        in_specs=[SMEM, VMEM, VMEM],
        out_specs=(VMEM,) * 4,
        scratch_shapes=[pltpu.VMEM((MATS * KV_ROWS, TILE), jnp.float32)] * 2,
        compiler_params=pltpu.CompilerParams(vmem_limit_bytes=24 << 20),
    )(place, partial, momentum)


def gram_kernel(place_ref, halves_ref, out_ref, rows):
    rows[:, :TILE] = halves_ref[0]
    rows[:, TILE:] = halves_ref[1]
    strip = place_ref[3]
    i, start = jnp.int32(0), jnp.int32(0)
    for begin, step in zip(STARTS[1:], np.diff(STARTS)):
        past = strip >= begin
        i += past.astype(jnp.int32)
        start += jnp.where(past, int(step), 0)
    j = 2 * (strip - start)
    ends = strip == 0
    sides = [(i, j), (jnp.where(ends, 8, i), jnp.where(ends, 8, j + 1))]
    for side, pair in enumerate(sides):
        left, right = (rows[pl.ds(pl.multiple_of(k * BLOCK, BLOCK), BLOCK), :] for k in pair)
        out_ref[:, side * BLOCK : (side + 1) * BLOCK] = lax.dot_general(
            left,
            right,
            NT,
            precision=lax.Precision.HIGHEST,
            preferred_element_type=jnp.float32,
        )


def gram(place, halves):
    return pl.pallas_call(
        gram_kernel,
        out_shape=jax.ShapeDtypeStruct((BLOCK, TILE), jnp.float32),
        in_specs=[SMEM, VMEM],
        out_specs=VMEM,
        scratch_shapes=[pltpu.VMEM((KV_ROWS, 2 * TILE), jnp.float32)],
        compiler_params=pltpu.CompilerParams(vmem_limit_bytes=24 << 20),
    )(place, halves)


def three(x):
    top = x.astype(jnp.bfloat16)
    rest = x - top.astype(jnp.float32)
    middle = rest.astype(jnp.bfloat16)
    bottom = (rest - middle.astype(jnp.float32)).astype(jnp.bfloat16)
    return top, middle, bottom


def times(x, right):
    n = x.shape[0]
    parts = three(x)
    total = 0.0
    for at, ref in reversed(list(enumerate(right))):
        product = lax.dot_general(
            jnp.concatenate(parts[: 3 - at], 0),
            ref[...],
            NN,
            preferred_element_type=jnp.float32,
        )
        for k in reversed(range(3 - at)):
            total = total + product[k * n : (k + 1) * n]
    return total


def triangle(strips_ref):
    zero = jnp.zeros((BLOCK, BLOCK), jnp.float32)
    strip = {}
    for at, ((i, j), other) in enumerate(STRIPS[1:], 1):
        strip[i, j // 2] = strips_ref[at]
    ends = strips_ref[0]
    strip[0, 0] = jnp.concatenate([ends[:, :BLOCK], strip[1, 0][:, :BLOCK].T], 1)
    strip[8, 4] = jnp.concatenate([ends[:, BLOCK:], zero], 1)
    blank = jnp.concatenate([zero, zero], 1)
    return {
        (i, j): jnp.concatenate([strip[2 * i, j], strip.get((2 * i + 1, j), blank)], 0)
        for i, j in PAIRS
    }


def chain_kernel(place_ref, strips_ref, halves_ref, out_ref, g0, g1, t0, t1, t2):
    first_row = place_ref[2]
    blocks = triangle(strips_ref)
    row = lax.broadcasted_iota(jnp.int32, (TILE, TILE), 0)
    column = lax.broadcasted_iota(jnp.int32, (TILE, TILE), 1)
    diagonal = jnp.zeros((TILE, TILE), jnp.float32)
    for i in range(5):
        diagonal += jnp.where(row == column, blocks[i, i], 0.0)
    squares = jnp.sum(jnp.sum(diagonal, axis=0, keepdims=True), axis=1, keepdims=True)
    scale = GAIN / (GAIN * jnp.sqrt(squares) + 1e-07)
    for i, j in PAIRS:
        block = (blocks[i, j] * scale) * scale
        here = (slice(i * TILE, (i + 1) * TILE), slice(j * TILE, (j + 1) * TILE))
        for ref, part in zip((g0, g1), three(block)):
            ref[here] = part
        if i != j:
            for ref, part in zip((g0, g1), three(block.T)):
                ref[here[1], here[0]] = part
    for half in range(2):
        for ref, part in zip((t0, t1, t2), three(halves_ref[half])):
            ref[:KV_ROWS, half * TILE : (half + 1) * TILE] = part
    for ref in (t0, t1, t2):
        ref[KV_ROWS:, :] = jnp.zeros((PADDED - KV_ROWS, 2 * TILE), jnp.bfloat16)
    g, t = (g0, g1), (t0, t1, t2)

    r = lax.broadcasted_iota(jnp.int32, (32, PADDED), 0)
    k = lax.broadcasted_iota(jnp.int32, (32, PADDED), 1)
    wanted = first_row + 144 * (r >> 3) + (r & 7)
    pick = jnp.where(jnp.logical_and(k == wanted, (r & 7) < 6), 1.0, 0.0)

    def poly(x):
        once = times(x, g)
        return coef_a * x + coef_b * once + coef_c * times(once, g)

    first = poly(pick)
    second = times(poly(poly(first)), g)
    third = times(poly(poly(second)), g)
    rows = coef_a * first + coef_b * second + coef_c * third
    gain = (0.2 * math.sqrt(max(KV_ROWS, D))) * scale
    update = gain * times(rows, t)
    own = times(pick, t)
    for x in range(4):
        out_ref[x, :8, :] = update[8 * x : 8 * x + 8]
        out_ref[x, 8:, :] = own[8 * x : 8 * x + 8]


def chain(place, strips, halves):
    return pl.pallas_call(
        chain_kernel,
        out_shape=jax.ShapeDtypeStruct((4, 16, 2 * TILE), jnp.float32),
        in_specs=[SMEM, VMEM, VMEM],
        out_specs=VMEM,
        scratch_shapes=[pltpu.VMEM((PADDED, PADDED), jnp.bfloat16)] * 2
        + [pltpu.VMEM((PADDED, 2 * TILE), jnp.bfloat16)] * 3,
        compiler_params=pltpu.CompilerParams(vmem_limit_bytes=24 << 20),
    )(place, strips, halves)


def finish_kernel(got_ref, momentum_ref, update_ref, new_ref, update_half, sum_half):
    for half in range(2):
        columns = slice(half * TILE, (half + 1) * TILE)
        for m in range(MATS):
            rows = pl.ds(m, 6, stride=MATS)
            update_half[rows, :] = got_ref[m, 0:6, columns]
            sum_half[rows, :] = got_ref[m, 8:14, columns]
        momentum = momentum_ref[:, columns]
        update_ref[:, columns] = update_half[...]
        new_ref[:, columns] = 0.95 * momentum + (sum_half[...] - KAPPA * momentum)


def finish(got, momentum):
    shape = jax.ShapeDtypeStruct(momentum.shape, jnp.float32)
    return pl.pallas_call(
        finish_kernel,
        out_shape=(shape, shape),
        in_specs=[VMEM, VMEM],
        out_specs=(VMEM, VMEM),
        scratch_shapes=[pltpu.VMEM((24, TILE), jnp.float32)] * 2,
    )(got, momentum)


def exchange(x, axis):
    return lax.all_to_all(x, axis, split_axis=0, concat_axis=0, tiled=True)


def spread(x, axis, count):
    return exchange(jnp.broadcast_to(x[None], (count, *x.shape)), axis)


def per_device(partials, momentum):
    w, v, x, c = (lax.axis_index(name) for name in ("w", "v", "x", "c"))
    z = 3 * w + v
    first_row = 48 * v + 12 * x + 6 * c
    strip = c * 12 + v * 4 + x
    place = jnp.stack([c, (z * 4 + x) * 2 + c, first_row, strip]).astype(jnp.int32)
    parts = split(place, partials[0], momentum)
    near = []
    for keep, send in zip(parts[:2], parts[2:]):
        got = lax.ppermute(send, "c", [(0, 1), (1, 0)])
        near.append(jnp.sum(exchange(keep + got, ("v", "x")), axis=0))
    own = jnp.sum(exchange(jnp.concatenate(near, 0), "w"), axis=0)
    half = spread(own, ("v", "x"), 12).reshape(KV_ROWS, TILE)
    halves = lax.all_gather(half, "c", axis=0, tiled=False)
    mine = jnp.sum(spread(gram(place, halves), "y", 8), axis=0)
    strips = lax.all_gather(spread(mine, ("v", "x"), 12), "c", axis=0, tiled=True)
    done = chain(place, strips, halves)
    return finish(exchange(done, "w"), momentum)


def solution(mesh):
    fine = Mesh(mesh.devices.reshape(4, 3, 4, 2, 8), ("w", "v", "x", "c", "y"))
    rows = ("w", "v", "x", "c")
    return jax.shard_map(
        per_device,
        mesh=fine,
        in_specs=(P(rows, None, "y"), P(rows, "y")),
        out_specs=(P(rows, "y"), P(rows, "y")),
        check_vma=False,
    )
```

```python
import functools
import math

import jax
import jax.numpy as jnp
import numpy as np
from jax import lax
from jax.experimental import pallas as pl
from jax.experimental.pallas import tpu as pltpu
from jax.sharding import Mesh
from jax.sharding import PartitionSpec as P

D = 2048
KV_ROWS = 576
MATS = 4
PADDED = 640
TILE = 128

coef_a = 3.4445
coef_b = -4.775
coef_c = 2.0315

GAIN = 1.95
KAPPA = 0.9025 / 1.95

BLOCK = 64

STRIPS = [((0, 0), (8, 8))]
STRIPS += [
    ((i, 2 * j), (i, 2 * j + 1))
    for i in range(1, 9)
    for j in range(i // 2 + 1)
    if (i, j) != (8, 4)
]
STARTS = [next(n for n, (a, _) in enumerate(STRIPS) if a[0] == i) for i in range(9)]
PAIRS = [(i, j) for i in range(5) for j in range(i + 1)]

CHUNKS = 4
SPLIT_LIMIT = 53739520

VMEM = pl.BlockSpec(memory_space=pltpu.VMEM)
HBM = pl.BlockSpec(memory_space=pltpu.HBM)
SMEM = pl.BlockSpec(memory_space=pltpu.SMEM)
NT = (((1,), (1,)), ((), ()))
NN = (((1,), (0,)), ((), ()))


def split_kernel(
    place_ref, partial_ref, momentum_ref, keep_ref, send_ref, raw, held, low, high, sems
):
    core, position = place_ref[0], place_ref[1]
    chunk = raw.shape[0] // CHUNKS
    copies = [pltpu.make_async_copy(momentum_ref, held, sems.at[CHUNKS])]
    for q in range(CHUNKS):
        rows = pl.ds(q * chunk, chunk)
        copies.append(pltpu.make_async_copy(partial_ref.at[rows], raw.at[rows], sems.at[q]))
    for copy in copies:
        copy.start()
    for q in range(CHUNKS):
        copies[q + 1].wait()
        rows = slice(q * chunk, (q + 1) * chunk)
        low[rows, :] = raw[rows, :TILE].astype(jnp.float32)
        high[rows, :] = raw[rows, TILE:].astype(jnp.float32)
    copies[0].wait()
    own = pl.ds(pl.multiple_of(position * 24, 8), 24)
    low[own, :] += KAPPA * held[:, :TILE]
    high[own, :] += KAPPA * held[:, TILE:]

    def put(mine, other):
        for m in range(MATS):
            rows = pl.ds(m, KV_ROWS, stride=MATS)
            keep_ref[:, m] = mine[rows, :].reshape(12, 48, TILE)
            send_ref[:, m] = other[rows, :].reshape(12, 48, TILE)

    @pl.when(core == 0)
    def _():
        put(low, high)

    @pl.when(core == 1)
    def _():
        put(high, low)


def split(place, partial, momentum):
    half = jax.ShapeDtypeStruct((12, MATS, 48, TILE), jnp.float32)
    return pl.pallas_call(
        split_kernel,
        out_shape=(half, half),
        in_specs=[SMEM, HBM, HBM],
        out_specs=(VMEM, VMEM),
        scratch_shapes=[
            pltpu.VMEM((MATS * KV_ROWS, 2 * TILE), jnp.bfloat16),
            pltpu.VMEM((24, 2 * TILE), jnp.float32),
        ]
        + [pltpu.VMEM((MATS * KV_ROWS, TILE), jnp.float32)] * 2
        + [pltpu.SemaphoreType.DMA((CHUNKS + 1,))],
        compiler_params=pltpu.CompilerParams(vmem_limit_bytes=SPLIT_LIMIT),
    )(place, partial, momentum)


def gram_kernel(place_ref, halves_ref, out_ref, rows):
    rows[:, :TILE] = halves_ref[0]
    rows[:, TILE:] = halves_ref[1]
    strip = place_ref[3]
    i, start = jnp.int32(0), jnp.int32(0)
    for begin, step in zip(STARTS[1:], np.diff(STARTS)):
        past = strip >= begin
        i += past.astype(jnp.int32)
        start += jnp.where(past, int(step), 0)
    j = 2 * (strip - start)
    ends = strip == 0
    sides = [(i, j), (jnp.where(ends, 8, i), jnp.where(ends, 8, j + 1))]
    for side, pair in enumerate(sides):
        left, right = (rows[pl.ds(pl.multiple_of(k * BLOCK, BLOCK), BLOCK), :] for k in pair)
        out_ref[:, side * BLOCK : (side + 1) * BLOCK] = lax.dot_general(
            left,
            right,
            NT,
            precision=lax.Precision.HIGHEST,
            preferred_element_type=jnp.float32,
        )


def gram(place, halves):
    return pl.pallas_call(
        gram_kernel,
        out_shape=jax.ShapeDtypeStruct((BLOCK, TILE), jnp.float32),
        in_specs=[SMEM, VMEM],
        out_specs=VMEM,
        scratch_shapes=[pltpu.VMEM((KV_ROWS, 2 * TILE), jnp.float32)],
        compiler_params=pltpu.CompilerParams(vmem_limit_bytes=24 << 20),
    )(place, halves)


def three(x):
    top = x.astype(jnp.bfloat16)
    rest = x - top.astype(jnp.float32)
    middle = rest.astype(jnp.bfloat16)
    bottom = (rest - middle.astype(jnp.float32)).astype(jnp.bfloat16)
    return top, middle, bottom


def times(x, right):
    n = x.shape[0]
    parts = three(x)
    total = 0.0
    for at, ref in reversed(list(enumerate(right))):
        product = lax.dot_general(
            jnp.concatenate(parts[: 3 - at], 0),
            ref[...],
            NN,
            preferred_element_type=jnp.float32,
        )
        for k in reversed(range(3 - at)):
            total = total + product[k * n : (k + 1) * n]
    return total


def triangle(strips_ref):
    zero = jnp.zeros((BLOCK, BLOCK), jnp.float32)
    strip = {}
    for at, ((i, j), other) in enumerate(STRIPS[1:], 1):
        strip[i, j // 2] = strips_ref[at]
    ends = strips_ref[0]
    strip[0, 0] = jnp.concatenate([ends[:, :BLOCK], strip[1, 0][:, :BLOCK].T], 1)
    strip[8, 4] = jnp.concatenate([ends[:, BLOCK:], zero], 1)
    blank = jnp.concatenate([zero, zero], 1)
    return {
        (i, j): jnp.concatenate([strip[2 * i, j], strip.get((2 * i + 1, j), blank)], 0)
        for i, j in PAIRS
    }


def chain_kernel(place_ref, strips_ref, halves_ref, out_ref, g0, g1, t0, t1, t2):
    first_row = place_ref[2]
    blocks = triangle(strips_ref)
    row = lax.broadcasted_iota(jnp.int32, (TILE, TILE), 0)
    column = lax.broadcasted_iota(jnp.int32, (TILE, TILE), 1)
    diagonal = jnp.zeros((TILE, TILE), jnp.float32)
    for i in range(5):
        diagonal += jnp.where(row == column, blocks[i, i], 0.0)
    squares = jnp.sum(jnp.sum(diagonal, axis=0, keepdims=True), axis=1, keepdims=True)
    scale = GAIN / (GAIN * jnp.sqrt(squares) + 1e-07)
    for i, j in PAIRS:
        block = (blocks[i, j] * scale) * scale
        here = (slice(i * TILE, (i + 1) * TILE), slice(j * TILE, (j + 1) * TILE))
        for ref, part in zip((g0, g1), three(block)):
            ref[here] = part
        if i != j:
            for ref, part in zip((g0, g1), three(block.T)):
                ref[here[1], here[0]] = part
    for half in range(2):
        for ref, part in zip((t0, t1, t2), three(halves_ref[half])):
            ref[:KV_ROWS, half * TILE : (half + 1) * TILE] = part
    for ref in (t0, t1, t2):
        ref[KV_ROWS:, :] = jnp.zeros((PADDED - KV_ROWS, 2 * TILE), jnp.bfloat16)
    g, t = (g0, g1), (t0, t1, t2)

    r = lax.broadcasted_iota(jnp.int32, (32, PADDED), 0)
    k = lax.broadcasted_iota(jnp.int32, (32, PADDED), 1)
    wanted = first_row + 144 * (r >> 3) + (r & 7)
    pick = jnp.where(jnp.logical_and(k == wanted, (r & 7) < 6), 1.0, 0.0)

    def poly(x):
        once = times(x, g)
        return coef_a * x + coef_b * once + coef_c * times(once, g)

    first = poly(pick)
    second = times(poly(poly(first)), g)
    third = times(poly(poly(second)), g)
    rows = coef_a * first + coef_b * second + coef_c * third
    gain = (0.2 * math.sqrt(max(KV_ROWS, D))) * scale
    both = times(jnp.concatenate([rows, pick], 0), t)
    update, own = gain * both[:32], both[32:]
    for x in range(4):
        out_ref[x, :8, :] = update[8 * x : 8 * x + 8]
        out_ref[x, 8:, :] = own[8 * x : 8 * x + 8]


def chain(place, strips, halves):
    return pl.pallas_call(
        chain_kernel,
        out_shape=jax.ShapeDtypeStruct((4, 16, 2 * TILE), jnp.float32),
        in_specs=[SMEM, VMEM, VMEM],
        out_specs=VMEM,
        scratch_shapes=[pltpu.VMEM((PADDED, PADDED), jnp.bfloat16)] * 2
        + [pltpu.VMEM((PADDED, 2 * TILE), jnp.bfloat16)] * 3,
        compiler_params=pltpu.CompilerParams(vmem_limit_bytes=24 << 20),
    )(place, strips, halves)


def finish_kernel(got_ref, momentum_ref, update_ref, new_ref, update_half, sum_half):
    for half in range(2):
        columns = slice(half * TILE, (half + 1) * TILE)
        for m in range(MATS):
            rows = pl.ds(m, 6, stride=MATS)
            update_half[rows, :] = got_ref[m, 0:6, columns]
            sum_half[rows, :] = got_ref[m, 8:14, columns]
        momentum = momentum_ref[:, columns]
        update_ref[:, columns] = update_half[...]
        new_ref[:, columns] = 0.95 * momentum + (sum_half[...] - KAPPA * momentum)


def finish(got, momentum):
    shape = jax.ShapeDtypeStruct(momentum.shape, jnp.float32)
    return pl.pallas_call(
        finish_kernel,
        out_shape=(shape, shape),
        in_specs=[VMEM, VMEM],
        out_specs=(VMEM, VMEM),
        scratch_shapes=[pltpu.VMEM((24, TILE), jnp.float32)] * 2,
        compiler_params=pltpu.CompilerParams(vmem_limit_bytes=4 << 20),
    )(got, momentum)


def exchange(x, axis):
    return lax.all_to_all(x, axis, split_axis=0, concat_axis=0, tiled=True)


def spread(x, axis, count):
    return exchange(jnp.broadcast_to(x[None], (count, *x.shape)), axis)


def per_device(partials, momentum):
    w, v, x, c = (lax.axis_index(name) for name in ("w", "v", "x", "c"))
    z = 3 * w + v
    first_row = 48 * v + 12 * x + 6 * c
    strip = c * 12 + v * 4 + x
    place = jnp.stack([c, (z * 4 + x) * 2 + c, first_row, strip]).astype(jnp.int32)
    keep, send = split(place, partials[0], momentum)
    got = lax.ppermute(send, "c", [(0, 1), (1, 0)])
    near = jnp.sum(exchange(keep + got, ("v", "x")), axis=0)
    own = jnp.sum(exchange(near, "w"), axis=0)
    half = spread(own, ("v", "x"), 12).reshape(KV_ROWS, TILE)
    halves = lax.all_gather(half, "c", axis=0, tiled=False)
    mine = jnp.sum(spread(gram(place, halves), "y", 8), axis=0)
    strips = lax.all_gather(spread(mine, ("v", "x"), 12), "c", axis=0, tiled=True)
    done = chain(place, strips, halves)
    return finish(exchange(done, "w"), momentum)


def solution(mesh):
    fine = Mesh(mesh.devices.reshape(4, 3, 4, 2, 8), ("w", "v", "x", "c", "y"))
    rows = ("w", "v", "x", "c")
    return jax.shard_map(
        per_device,
        mesh=fine,
        in_specs=(P(rows, None, "y"), P(rows, "y")),
        out_specs=(P(rows, "y"), P(rows, "y")),
        check_vma=False,
    )
```

```python
import functools
import math

import jax
import jax.numpy as jnp
import numpy as np
from jax import lax
from jax.experimental import pallas as pl
from jax.experimental.pallas import tpu as pltpu
from jax.sharding import Mesh
from jax.sharding import PartitionSpec as P

D = 2048
KV_ROWS = 576
MATS = 4
PADDED = 640
TILE = 128

coef_a = 3.4445
coef_b = -4.775
coef_c = 2.0315

GAIN = 1.95
KAPPA = 0.9025 / 1.95

BLOCK = 64

STRIPS = [((0, 0), (8, 8))]
STRIPS += [
    ((i, 2 * j), (i, 2 * j + 1))
    for i in range(1, 9)
    for j in range(i // 2 + 1)
    if (i, j) != (8, 4)
]
STARTS = [next(n for n, (a, _) in enumerate(STRIPS) if a[0] == i) for i in range(9)]
PAIRS = [(i, j) for i in range(5) for j in range(i + 1)]

CHUNKS = 4
SPLIT_LIMIT = 53739520

VMEM = pl.BlockSpec(memory_space=pltpu.VMEM)
HBM = pl.BlockSpec(memory_space=pltpu.HBM)
SMEM = pl.BlockSpec(memory_space=pltpu.SMEM)
NT = (((1,), (1,)), ((), ()))
NN = (((1,), (0,)), ((), ()))


def split_kernel(
    place_ref, partial_ref, momentum_ref, keep_ref, send_ref, raw, held, low, high, sems
):
    core, position = place_ref[0], place_ref[1]
    chunk = raw.shape[0] // CHUNKS
    copies = [pltpu.make_async_copy(momentum_ref, held, sems.at[CHUNKS])]
    for q in range(CHUNKS):
        rows = pl.ds(q * chunk, chunk)
        copies.append(pltpu.make_async_copy(partial_ref.at[rows], raw.at[rows], sems.at[q]))
    for copy in copies:
        copy.start()
    copies[0].wait()
    own = position * 24
    for q in range(CHUNKS):
        copies[q + 1].wait()
        rows = slice(q * chunk, (q + 1) * chunk)
        low[rows, :] = raw[rows, :TILE].astype(jnp.float32)
        high[rows, :] = raw[rows, TILE:].astype(jnp.float32)

        @pl.when(own // chunk == q)
        def _():
            mine = pl.ds(pl.multiple_of(own, 8), 24)
            low[mine, :] += KAPPA * held[:, :TILE]
            high[mine, :] += KAPPA * held[:, TILE:]

        def put(mine, other):
            for m in range(MATS):
                rows = pl.ds(q * chunk + m, chunk // MATS, stride=MATS)
                groups = slice(q * 12 // CHUNKS, (q + 1) * 12 // CHUNKS)
                keep_ref[groups, m] = mine[rows, :].reshape(-1, 48, TILE)
                send_ref[groups, m] = other[rows, :].reshape(-1, 48, TILE)

        @pl.when(core == 0)
        def _():
            put(low, high)

        @pl.when(core == 1)
        def _():
            put(high, low)


def split(place, partial, momentum):
    half = jax.ShapeDtypeStruct((12, MATS, 48, TILE), jnp.float32)
    return pl.pallas_call(
        split_kernel,
        out_shape=(half, half),
        in_specs=[SMEM, HBM, HBM],
        out_specs=(VMEM, VMEM),
        scratch_shapes=[
            pltpu.VMEM((MATS * KV_ROWS, 2 * TILE), jnp.bfloat16),
            pltpu.VMEM((24, 2 * TILE), jnp.float32),
        ]
        + [pltpu.VMEM((MATS * KV_ROWS, TILE), jnp.float32)] * 2
        + [pltpu.SemaphoreType.DMA((CHUNKS + 1,))],
        compiler_params=pltpu.CompilerParams(vmem_limit_bytes=SPLIT_LIMIT),
    )(place, partial, momentum)


def gram_kernel(place_ref, halves_ref, out_ref):
    strip = place_ref[3]
    i, start = jnp.int32(0), jnp.int32(0)
    for begin, step in zip(STARTS[1:], np.diff(STARTS)):
        past = strip >= begin
        i += past.astype(jnp.int32)
        start += jnp.where(past, int(step), 0)
    j = 2 * (strip - start)
    ends = strip == 0
    sides = [(i, j), (jnp.where(ends, 8, i), jnp.where(ends, 8, j + 1))]
    for side, pair in enumerate(sides):
        picks = [pl.ds(pl.multiple_of(k * BLOCK, BLOCK), BLOCK) for k in pair]
        left, right = (
            jnp.concatenate([halves_ref[0, rows, :], halves_ref[1, rows, :]], 1) for rows in picks
        )
        out_ref[:, side * BLOCK : (side + 1) * BLOCK] = lax.dot_general(
            left,
            right,
            NT,
            precision=lax.Precision.HIGHEST,
            preferred_element_type=jnp.float32,
        )


def gram(place, halves):
    return pl.pallas_call(
        gram_kernel,
        out_shape=jax.ShapeDtypeStruct((BLOCK, TILE), jnp.float32),
        in_specs=[SMEM, VMEM],
        out_specs=VMEM,
        compiler_params=pltpu.CompilerParams(vmem_limit_bytes=24 << 20),
    )(place, halves)


def three(x):
    top = x.astype(jnp.bfloat16)
    rest = x - top.astype(jnp.float32)
    middle = rest.astype(jnp.bfloat16)
    bottom = (rest - middle.astype(jnp.float32)).astype(jnp.bfloat16)
    return top, middle, bottom


def times(x, right):
    n = x.shape[0]
    parts = three(x)
    total = 0.0
    for at, ref in reversed(list(enumerate(right))):
        product = lax.dot_general(
            jnp.concatenate(parts[: 3 - at], 0),
            ref[...],
            NN,
            preferred_element_type=jnp.float32,
        )
        for k in reversed(range(3 - at)):
            total = total + product[k * n : (k + 1) * n]
    return total


def triangle(strips_ref):
    zero = jnp.zeros((BLOCK, BLOCK), jnp.float32)
    strip = {}
    for at, ((i, j), other) in enumerate(STRIPS[1:], 1):
        strip[i, j // 2] = strips_ref[at]
    ends = strips_ref[0]
    strip[0, 0] = jnp.concatenate([ends[:, :BLOCK], strip[1, 0][:, :BLOCK].T], 1)
    strip[8, 4] = jnp.concatenate([ends[:, BLOCK:], zero], 1)
    blank = jnp.concatenate([zero, zero], 1)
    return {
        (i, j): jnp.concatenate([strip[2 * i, j], strip.get((2 * i + 1, j), blank)], 0)
        for i, j in PAIRS
    }


def chain_kernel(place_ref, strips_ref, halves_ref, out_ref, g0, g1, t0, t1, t2):
    first_row = place_ref[2]
    blocks = triangle(strips_ref)
    row = lax.broadcasted_iota(jnp.int32, (TILE, TILE), 0)
    column = lax.broadcasted_iota(jnp.int32, (TILE, TILE), 1)
    diagonal = jnp.zeros((TILE, TILE), jnp.float32)
    for i in range(5):
        diagonal += jnp.where(row == column, blocks[i, i], 0.0)
    squares = jnp.sum(jnp.sum(diagonal, axis=0, keepdims=True), axis=1, keepdims=True)
    scale = GAIN / (GAIN * jnp.sqrt(squares) + 1e-07)
    for i, j in PAIRS:
        block = (blocks[i, j] * scale) * scale
        here = (slice(i * TILE, (i + 1) * TILE), slice(j * TILE, (j + 1) * TILE))
        for ref, part in zip((g0, g1), three(block)):
            ref[here] = part
        if i != j:
            for ref, part in zip((g0, g1), three(block.T)):
                ref[here[1], here[0]] = part
    for half in range(2):
        for ref, part in zip((t0, t1, t2), three(halves_ref[half])):
            ref[:KV_ROWS, half * TILE : (half + 1) * TILE] = part
    for ref in (t0, t1, t2):
        ref[KV_ROWS:, :] = jnp.zeros((PADDED - KV_ROWS, 2 * TILE), jnp.bfloat16)
    g, t = (g0, g1), (t0, t1, t2)

    r = lax.broadcasted_iota(jnp.int32, (32, PADDED), 0)
    k = lax.broadcasted_iota(jnp.int32, (32, PADDED), 1)
    wanted = first_row + 144 * (r >> 3) + (r & 7)
    pick = jnp.where(jnp.logical_and(k == wanted, (r & 7) < 6), 1.0, 0.0)

    def poly(x):
        once = times(x, g)
        return coef_a * x + coef_b * once + coef_c * times(once, g)

    first = poly(pick)
    second = times(poly(poly(first)), g)
    third = times(poly(poly(second)), g)
    rows = coef_a * first + coef_b * second + coef_c * third
    gain = (0.2 * math.sqrt(max(KV_ROWS, D))) * scale
    both = times(jnp.concatenate([rows, pick], 0), t)
    update, own = gain * both[:32], both[32:]
    for x in range(4):
        out_ref[x, :8, :] = update[8 * x : 8 * x + 8]
        out_ref[x, 8:, :] = own[8 * x : 8 * x + 8]


def chain(place, strips, halves):
    return pl.pallas_call(
        chain_kernel,
        out_shape=jax.ShapeDtypeStruct((4, 16, 2 * TILE), jnp.float32),
        in_specs=[SMEM, VMEM, VMEM],
        out_specs=VMEM,
        scratch_shapes=[pltpu.VMEM((PADDED, PADDED), jnp.bfloat16)] * 2
        + [pltpu.VMEM((PADDED, 2 * TILE), jnp.bfloat16)] * 3,
        compiler_params=pltpu.CompilerParams(vmem_limit_bytes=24 << 20),
    )(place, strips, halves)


def finish_kernel(got_ref, momentum_ref, update_ref, new_ref, update_half, sum_half):
    for half in range(2):
        columns = slice(half * TILE, (half + 1) * TILE)
        for m in range(MATS):
            rows = pl.ds(m, 6, stride=MATS)
            update_half[rows, :] = got_ref[m, 0:6, columns]
            sum_half[rows, :] = got_ref[m, 8:14, columns]
        momentum = momentum_ref[:, columns]
        update_ref[:, columns] = update_half[...]
        new_ref[:, columns] = 0.95 * momentum + (sum_half[...] - KAPPA * momentum)


def finish(got, momentum):
    shape = jax.ShapeDtypeStruct(momentum.shape, jnp.float32)
    return pl.pallas_call(
        finish_kernel,
        out_shape=(shape, shape),
        in_specs=[VMEM, VMEM],
        out_specs=(VMEM, VMEM),
        scratch_shapes=[pltpu.VMEM((24, TILE), jnp.float32)] * 2,
        compiler_params=pltpu.CompilerParams(vmem_limit_bytes=4 << 20),
    )(got, momentum)


def exchange(x, axis):
    return lax.all_to_all(x, axis, split_axis=0, concat_axis=0, tiled=True)


def spread(x, axis, count):
    return exchange(jnp.broadcast_to(x[None], (count, *x.shape)), axis)


def per_device(partials, momentum):
    w, v, x, c = (lax.axis_index(name) for name in ("w", "v", "x", "c"))
    z = 3 * w + v
    first_row = 48 * v + 12 * x + 6 * c
    strip = c * 12 + v * 4 + x
    place = jnp.stack([c, (z * 4 + x) * 2 + c, first_row, strip]).astype(jnp.int32)
    keep, send = split(place, partials[0], momentum)
    got = lax.ppermute(send, "c", [(0, 1), (1, 0)])
    near = jnp.sum(exchange(keep + got, ("v", "x")), axis=0)
    own = jnp.sum(exchange(near, "w"), axis=0)
    half = spread(own, ("v", "x"), 12).reshape(KV_ROWS, TILE)
    halves = lax.all_gather(half, "c", axis=0, tiled=False)
    mine = jnp.sum(spread(gram(place, halves), "y", 8), axis=0)
    strips = lax.all_gather(spread(mine, ("v", "x"), 12), "c", axis=0, tiled=True)
    done = chain(place, strips, halves)
    return finish(exchange(done, "w"), momentum)


def solution(mesh):
    fine = Mesh(mesh.devices.reshape(4, 3, 4, 2, 8), ("w", "v", "x", "c", "y"))
    rows = ("w", "v", "x", "c")
    return jax.shard_map(
        per_device,
        mesh=fine,
        in_specs=(P(rows, None, "y"), P(rows, "y")),
        out_specs=(P(rows, "y"), P(rows, "y")),
        check_vma=False,
    )
```

```python
import functools
import math

import jax
import jax.numpy as jnp
import numpy as np
from jax import lax
from jax.experimental import pallas as pl
from jax.experimental.pallas import tpu as pltpu
from jax.sharding import Mesh
from jax.sharding import PartitionSpec as P

D = 2048
KV_ROWS = 576
MATS = 4
PADDED = 640
TILE = 128

coef_a = 3.4445
coef_b = -4.775
coef_c = 2.0315

GAIN = 1.95
KAPPA = 0.9025 / 1.95

BLOCK = 64

STRIPS = [((0, 0), (8, 8))]
STRIPS += [
    ((i, 2 * j), (i, 2 * j + 1))
    for i in range(1, 9)
    for j in range(i // 2 + 1)
    if (i, j) != (8, 4)
]
STARTS = [next(n for n, (a, _) in enumerate(STRIPS) if a[0] == i) for i in range(9)]
PAIRS = [(i, j) for i in range(5) for j in range(i + 1)]

CHUNKS = 4
SPLIT_LIMIT = 53739520

VMEM = pl.BlockSpec(memory_space=pltpu.VMEM)
HBM = pl.BlockSpec(memory_space=pltpu.HBM)
SMEM = pl.BlockSpec(memory_space=pltpu.SMEM)
NT = (((1,), (1,)), ((), ()))
NN = (((1,), (0,)), ((), ()))


def split_kernel(
    place_ref, partial_ref, momentum_ref, keep_ref, send_ref, raw, held, low, high, sems
):
    core, position = place_ref[0], place_ref[1]
    chunk = raw.shape[0] // CHUNKS
    copies = [pltpu.make_async_copy(momentum_ref, held, sems.at[CHUNKS])]
    for q in range(CHUNKS):
        rows = pl.ds(q * chunk, chunk)
        copies.append(pltpu.make_async_copy(partial_ref.at[rows], raw.at[rows], sems.at[q]))
    for copy in copies:
        copy.start()
    copies[0].wait()
    own = position * 24
    for q in range(CHUNKS):
        copies[q + 1].wait()
        rows = slice(q * chunk, (q + 1) * chunk)
        low[rows, :] = raw[rows, :TILE].astype(jnp.float32)
        high[rows, :] = raw[rows, TILE:].astype(jnp.float32)

        @pl.when(own // chunk == q)
        def _():
            mine = pl.ds(pl.multiple_of(own, 8), 24)
            low[mine, :] += KAPPA * held[:, :TILE]
            high[mine, :] += KAPPA * held[:, TILE:]

        def put(mine, other):
            for m in range(MATS):
                rows = pl.ds(q * chunk + m, chunk // MATS, stride=MATS)
                groups = slice(q * 12 // CHUNKS, (q + 1) * 12 // CHUNKS)
                keep_ref[groups, m] = mine[rows, :].reshape(-1, 48, TILE)
                send_ref[groups, m] = other[rows, :].reshape(-1, 48, TILE)

        @pl.when(core == 0)
        def _():
            put(low, high)

        @pl.when(core == 1)
        def _():
            put(high, low)


def split(place, partial, momentum):
    half = jax.ShapeDtypeStruct((12, MATS, 48, TILE), jnp.float32)
    return pl.pallas_call(
        split_kernel,
        out_shape=(half, half),
        in_specs=[SMEM, HBM, HBM],
        out_specs=(VMEM, VMEM),
        scratch_shapes=[
            pltpu.VMEM((MATS * KV_ROWS, 2 * TILE), jnp.bfloat16),
            pltpu.VMEM((24, 2 * TILE), jnp.float32),
        ]
        + [pltpu.VMEM((MATS * KV_ROWS, TILE), jnp.float32)] * 2
        + [pltpu.SemaphoreType.DMA((CHUNKS + 1,))],
        compiler_params=pltpu.CompilerParams(vmem_limit_bytes=SPLIT_LIMIT),
    )(place, partial, momentum)


def gram_kernel(place_ref, halves_ref, out_ref):
    strip = place_ref[3]
    i, start = jnp.int32(0), jnp.int32(0)
    for begin, step in zip(STARTS[1:], np.diff(STARTS)):
        past = strip >= begin
        i += past.astype(jnp.int32)
        start += jnp.where(past, int(step), 0)
    j = 2 * (strip - start)
    ends = strip == 0
    sides = [(i, j), (jnp.where(ends, 8, i), jnp.where(ends, 8, j + 1))]
    for side, pair in enumerate(sides):
        picks = [pl.ds(pl.multiple_of(k * BLOCK, BLOCK), BLOCK) for k in pair]
        left, right = (
            jnp.concatenate([halves_ref[0, rows, :], halves_ref[1, rows, :]], 1) for rows in picks
        )
        left_top, left_middle, _ = three(left)
        right_top, right_middle, _ = three(right)
        dot = functools.partial(
            lax.dot_general, dimension_numbers=NT, preferred_element_type=jnp.float32
        )
        both = dot(jnp.concatenate([left_top, left_middle], 0), right_top)
        small = both[BLOCK:] + dot(left_top, right_middle)
        out_ref[:, side * BLOCK : (side + 1) * BLOCK] = both[:BLOCK] + small


def gram(place, halves):
    return pl.pallas_call(
        gram_kernel,
        out_shape=jax.ShapeDtypeStruct((BLOCK, TILE), jnp.float32),
        in_specs=[SMEM, VMEM],
        out_specs=VMEM,
        compiler_params=pltpu.CompilerParams(vmem_limit_bytes=24 << 20),
    )(place, halves)


def three(x):
    top = x.astype(jnp.bfloat16)
    rest = x - top.astype(jnp.float32)
    middle = rest.astype(jnp.bfloat16)
    bottom = (rest - middle.astype(jnp.float32)).astype(jnp.bfloat16)
    return top, middle, bottom


def times(x, right):
    n, count = x.shape[0], len(right)
    parts = three(x)
    total = 0.0
    for at, ref in reversed(list(enumerate(right))):
        product = lax.dot_general(
            jnp.concatenate(parts[: count - at], 0),
            ref[...],
            NN,
            preferred_element_type=jnp.float32,
        )
        for k in reversed(range(count - at)):
            total = total + product[k * n : (k + 1) * n]
    return total


def triangle(strips_ref):
    zero = jnp.zeros((BLOCK, BLOCK), jnp.float32)
    strip = {}
    for at, ((i, j), other) in enumerate(STRIPS[1:], 1):
        strip[i, j // 2] = strips_ref[at]
    ends = strips_ref[0]
    strip[0, 0] = jnp.concatenate([ends[:, :BLOCK], strip[1, 0][:, :BLOCK].T], 1)
    strip[8, 4] = jnp.concatenate([ends[:, BLOCK:], zero], 1)
    blank = jnp.concatenate([zero, zero], 1)
    return {
        (i, j): jnp.concatenate([strip[2 * i, j], strip.get((2 * i + 1, j), blank)], 0)
        for i, j in PAIRS
    }


def chain_kernel(place_ref, strips_ref, halves_ref, out_ref, g0, g1, t0, t1, t2):
    first_row = place_ref[2]
    blocks = triangle(strips_ref)
    row = lax.broadcasted_iota(jnp.int32, (TILE, TILE), 0)
    column = lax.broadcasted_iota(jnp.int32, (TILE, TILE), 1)
    diagonal = jnp.zeros((TILE, TILE), jnp.float32)
    for i in range(5):
        diagonal += jnp.where(row == column, blocks[i, i], 0.0)
    squares = jnp.sum(jnp.sum(diagonal, axis=0, keepdims=True), axis=1, keepdims=True)
    scale = GAIN / (GAIN * jnp.sqrt(squares) + 1e-07)
    for i, j in PAIRS:
        block = (blocks[i, j] * scale) * scale
        here = (slice(i * TILE, (i + 1) * TILE), slice(j * TILE, (j + 1) * TILE))
        for ref, part in zip((g0, g1), three(block)):
            ref[here] = part
        if i != j:
            for ref, part in zip((g0, g1), three(block.T)):
                ref[here[1], here[0]] = part
    for half in range(2):
        for ref, part in zip((t0, t1, t2), three(halves_ref[half])):
            ref[:KV_ROWS, half * TILE : (half + 1) * TILE] = part
    for ref in (t0, t1, t2):
        ref[KV_ROWS:, :] = jnp.zeros((PADDED - KV_ROWS, 2 * TILE), jnp.bfloat16)
    g, t = (g0, g1), (t0, t1, t2)

    r = lax.broadcasted_iota(jnp.int32, (32, PADDED), 0)
    k = lax.broadcasted_iota(jnp.int32, (32, PADDED), 1)
    wanted = first_row + 144 * (r >> 3) + (r & 7)
    pick = jnp.where(jnp.logical_and(k == wanted, (r & 7) < 6), 1.0, 0.0)

    def poly(x):
        once = times(x, g)
        return coef_a * x + coef_b * once + coef_c * times(once, g)

    first = poly(pick)
    second = times(poly(poly(first)), g)
    third = times(poly(poly(second)), g)
    rows = coef_a * first + coef_b * second + coef_c * third
    gain = (0.2 * math.sqrt(max(KV_ROWS, D))) * scale
    both = times(jnp.concatenate([rows, pick], 0), t)
    update, own = gain * both[:32], both[32:]
    for x in range(4):
        out_ref[x, :8, :] = update[8 * x : 8 * x + 8]
        out_ref[x, 8:, :] = own[8 * x : 8 * x + 8]


def chain(place, strips, halves):
    return pl.pallas_call(
        chain_kernel,
        out_shape=jax.ShapeDtypeStruct((4, 16, 2 * TILE), jnp.float32),
        in_specs=[SMEM, VMEM, VMEM],
        out_specs=VMEM,
        scratch_shapes=[pltpu.VMEM((PADDED, PADDED), jnp.bfloat16)] * 2
        + [pltpu.VMEM((PADDED, 2 * TILE), jnp.bfloat16)] * 3,
        compiler_params=pltpu.CompilerParams(vmem_limit_bytes=24 << 20),
    )(place, strips, halves)


def finish_kernel(got_ref, momentum_ref, update_ref, new_ref, update_half, sum_half):
    for half in range(2):
        columns = slice(half * TILE, (half + 1) * TILE)
        for m in range(MATS):
            rows = pl.ds(m, 6, stride=MATS)
            update_half[rows, :] = got_ref[m, 0:6, columns]
            sum_half[rows, :] = got_ref[m, 8:14, columns]
        momentum = momentum_ref[:, columns]
        update_ref[:, columns] = update_half[...]
        new_ref[:, columns] = 0.95 * momentum + (sum_half[...] - KAPPA * momentum)


def finish(got, momentum):
    shape = jax.ShapeDtypeStruct(momentum.shape, jnp.float32)
    return pl.pallas_call(
        finish_kernel,
        out_shape=(shape, shape),
        in_specs=[VMEM, VMEM],
        out_specs=(VMEM, VMEM),
        scratch_shapes=[pltpu.VMEM((24, TILE), jnp.float32)] * 2,
        compiler_params=pltpu.CompilerParams(vmem_limit_bytes=4 << 20),
    )(got, momentum)


def exchange(x, axis):
    return lax.all_to_all(x, axis, split_axis=0, concat_axis=0, tiled=True)


def spread(x, axis, count):
    return exchange(jnp.broadcast_to(x[None], (count, *x.shape)), axis)


def per_device(partials, momentum):
    w, v, x, c = (lax.axis_index(name) for name in ("w", "v", "x", "c"))
    z = 3 * w + v
    first_row = 48 * v + 12 * x + 6 * c
    strip = c * 12 + v * 4 + x
    place = jnp.stack([c, (z * 4 + x) * 2 + c, first_row, strip]).astype(jnp.int32)
    keep, send = split(place, partials[0], momentum)
    got = lax.ppermute(send, "c", [(0, 1), (1, 0)])
    near = jnp.sum(exchange(keep + got, ("v", "x")), axis=0)
    own = jnp.sum(exchange(near, "w"), axis=0)
    half = spread(own, ("v", "x"), 12).reshape(KV_ROWS, TILE)
    halves = lax.all_gather(half, "c", axis=0, tiled=False)
    mine = jnp.sum(spread(gram(place, halves), "y", 8), axis=0)
    strips = lax.all_gather(spread(mine, ("v", "x"), 12), "c", axis=0, tiled=True)
    done = chain(place, strips, halves)
    return finish(exchange(done, "w"), momentum)


def solution(mesh):
    fine = Mesh(mesh.devices.reshape(4, 3, 4, 2, 8), ("w", "v", "x", "c", "y"))
    rows = ("w", "v", "x", "c")
    return jax.shard_map(
        per_device,
        mesh=fine,
        in_specs=(P(rows, None, "y"), P(rows, "y")),
        out_specs=(P(rows, "y"), P(rows, "y")),
        check_vma=False,
    )
```

```python
import functools
import math

import jax
import jax.numpy as jnp
import numpy as np
from jax import lax
from jax.experimental import pallas as pl
from jax.experimental.pallas import tpu as pltpu
from jax.sharding import Mesh
from jax.sharding import PartitionSpec as P

D = 2048
KV_ROWS = 576
MATS = 4
PADDED = 640
TILE = 128

coef_a = 3.4445
coef_b = -4.775
coef_c = 2.0315

GAIN = 1.95
KAPPA = 0.9025 / 1.95

BLOCK = 64

STRIPS = [((0, 0), (8, 8))]
STRIPS += [
    ((i, 2 * j), (i, 2 * j + 1))
    for i in range(1, 9)
    for j in range(i // 2 + 1)
    if (i, j) != (8, 4)
]
STARTS = [next(n for n, (a, _) in enumerate(STRIPS) if a[0] == i) for i in range(9)]
PAIRS = [(i, j) for i in range(5) for j in range(i + 1)]

CHUNKS = 4
SPLIT_LIMIT = 53739520

VMEM = pl.BlockSpec(memory_space=pltpu.VMEM)
HBM = pl.BlockSpec(memory_space=pltpu.HBM)
SMEM = pl.BlockSpec(memory_space=pltpu.SMEM)
NT = (((1,), (1,)), ((), ()))
NN = (((1,), (0,)), ((), ()))


def split_kernel(
    place_ref, partial_ref, momentum_ref, keep_ref, send_ref, raw, held, low, high, sems
):
    core, position = place_ref[0], place_ref[1]
    chunk = raw.shape[0] // CHUNKS
    copies = [pltpu.make_async_copy(momentum_ref, held, sems.at[CHUNKS])]
    for q in range(CHUNKS):
        rows = pl.ds(q * chunk, chunk)
        copies.append(pltpu.make_async_copy(partial_ref.at[rows], raw.at[rows], sems.at[q]))
    for copy in copies:
        copy.start()
    copies[0].wait()
    own = position * 24
    for q in range(CHUNKS):
        copies[q + 1].wait()
        rows = slice(q * chunk, (q + 1) * chunk)
        low[rows, :] = raw[rows, :TILE].astype(jnp.float32)
        high[rows, :] = raw[rows, TILE:].astype(jnp.float32)

        @pl.when(own // chunk == q)
        def _():
            mine = pl.ds(pl.multiple_of(own, 8), 24)
            low[mine, :] += KAPPA * held[:, :TILE]
            high[mine, :] += KAPPA * held[:, TILE:]

        def put(mine, other):
            for m in range(MATS):
                rows = pl.ds(q * chunk + m, chunk // MATS, stride=MATS)
                groups = slice(q * 12 // CHUNKS, (q + 1) * 12 // CHUNKS)
                keep_ref[groups, m] = mine[rows, :].reshape(-1, 48, TILE)
                send_ref[groups, m] = other[rows, :].reshape(-1, 48, TILE)

        @pl.when(core == 0)
        def _():
            put(low, high)

        @pl.when(core == 1)
        def _():
            put(high, low)


def split(place, partial, momentum):
    half = jax.ShapeDtypeStruct((12, MATS, 48, TILE), jnp.float32)
    return pl.pallas_call(
        split_kernel,
        out_shape=(half, half),
        in_specs=[SMEM, HBM, HBM],
        out_specs=(VMEM, VMEM),
        scratch_shapes=[
            pltpu.VMEM((MATS * KV_ROWS, 2 * TILE), jnp.bfloat16),
            pltpu.VMEM((24, 2 * TILE), jnp.float32),
        ]
        + [pltpu.VMEM((MATS * KV_ROWS, TILE), jnp.float32)] * 2
        + [pltpu.SemaphoreType.DMA((CHUNKS + 1,))],
        compiler_params=pltpu.CompilerParams(vmem_limit_bytes=SPLIT_LIMIT),
    )(place, partial, momentum)


def gram_kernel(place_ref, halves_ref, out_ref):
    strip = place_ref[3]
    i, start = jnp.int32(0), jnp.int32(0)
    for begin, step in zip(STARTS[1:], np.diff(STARTS)):
        past = strip >= begin
        i += past.astype(jnp.int32)
        start += jnp.where(past, int(step), 0)
    j = 2 * (strip - start)
    ends = strip == 0
    sides = [(i, j), (jnp.where(ends, 8, i), jnp.where(ends, 8, j + 1))]
    for side, pair in enumerate(sides):
        picks = [pl.ds(pl.multiple_of(k * BLOCK, BLOCK), BLOCK) for k in pair]
        left, right = (
            jnp.concatenate([halves_ref[0, rows, :], halves_ref[1, rows, :]], 1) for rows in picks
        )
        left_top, left_middle, _ = three(left)
        right_top, right_middle, _ = three(right)
        dot = functools.partial(
            lax.dot_general, dimension_numbers=NT, preferred_element_type=jnp.float32
        )
        both = dot(jnp.concatenate([left_top, left_middle], 0), right_top)
        small = both[BLOCK:] + dot(left_top, right_middle)
        out_ref[:, side * BLOCK : (side + 1) * BLOCK] = both[:BLOCK] + small


def gram(place, halves):
    return pl.pallas_call(
        gram_kernel,
        out_shape=jax.ShapeDtypeStruct((BLOCK, TILE), jnp.float32),
        in_specs=[SMEM, VMEM],
        out_specs=VMEM,
        compiler_params=pltpu.CompilerParams(vmem_limit_bytes=24 << 20),
    )(place, halves)


def three(x):
    top = x.astype(jnp.bfloat16)
    rest = x - top.astype(jnp.float32)
    middle = rest.astype(jnp.bfloat16)
    bottom = (rest - middle.astype(jnp.float32)).astype(jnp.bfloat16)
    return top, middle, bottom


def times(x, right):
    n, count = x.shape[0], len(right)
    parts = three(x)
    total = 0.0
    for at, ref in reversed(list(enumerate(right))):
        product = lax.dot_general(
            jnp.concatenate(parts[: count - at], 0),
            ref[...],
            NN,
            preferred_element_type=jnp.float32,
        )
        for k in reversed(range(count - at)):
            total = total + product[k * n : (k + 1) * n]
    return total


def triangle(strips_ref):
    zero = jnp.zeros((BLOCK, BLOCK), jnp.float32)
    strip = {}
    for at, ((i, j), other) in enumerate(STRIPS[1:], 1):
        strip[i, j // 2] = strips_ref[at]
    ends = strips_ref[0]
    strip[0, 0] = jnp.concatenate([ends[:, :BLOCK], strip[1, 0][:, :BLOCK].T], 1)
    strip[8, 4] = jnp.concatenate([ends[:, BLOCK:], zero], 1)
    blank = jnp.concatenate([zero, zero], 1)
    return {
        (i, j): jnp.concatenate([strip[2 * i, j], strip.get((2 * i + 1, j), blank)], 0)
        for i, j in PAIRS
    }


def chain_kernel(place_ref, strips_ref, halves_ref, out_ref, g0, g1, t0, t1, t2):
    first_row = place_ref[2]
    blocks = triangle(strips_ref)
    row = lax.broadcasted_iota(jnp.int32, (TILE, TILE), 0)
    column = lax.broadcasted_iota(jnp.int32, (TILE, TILE), 1)
    diagonal = jnp.zeros((TILE, TILE), jnp.float32)
    for i in range(5):
        diagonal += jnp.where(row == column, blocks[i, i], 0.0)
    squares = jnp.sum(jnp.sum(diagonal, axis=0, keepdims=True), axis=1, keepdims=True)
    scale = GAIN / (GAIN * jnp.sqrt(squares) + 1e-07)
    for i, j in PAIRS:
        block = (blocks[i, j] * scale) * scale
        here = (slice(i * TILE, (i + 1) * TILE), slice(j * TILE, (j + 1) * TILE))
        for ref, part in zip((g0, g1), three(block)):
            ref[here] = part
        if i != j:
            for ref, part in zip((g0, g1), three(block.T)):
                ref[here[1], here[0]] = part
    for half in range(2):
        for ref, part in zip((t0, t1, t2), three(halves_ref[half])):
            ref[:KV_ROWS, half * TILE : (half + 1) * TILE] = part
    for ref in (t0, t1, t2):
        ref[KV_ROWS:, :] = jnp.zeros((PADDED - KV_ROWS, 2 * TILE), jnp.bfloat16)
    g, t = (g0, g1), (t0, t1, t2)

    r = lax.broadcasted_iota(jnp.int32, (32, PADDED), 0)
    k = lax.broadcasted_iota(jnp.int32, (32, PADDED), 1)
    wanted = first_row + 144 * (r >> 3) + (r & 7)
    pick = jnp.where(jnp.logical_and(k == wanted, (r & 7) < 6), 1.0, 0.0)

    def poly(x):
        once = times(x, g)
        return coef_a * x + coef_b * once + coef_c * times(once, g)

    first = poly(pick)
    second = times(poly(poly(first)), g)
    third = times(poly(poly(second)), g)
    rows = coef_a * first + coef_b * second + coef_c * third
    gain = (0.2 * math.sqrt(max(KV_ROWS, D))) * scale
    both = times(jnp.concatenate([rows, pick], 0), t)
    update, own = gain * both[:32], both[32:]
    for x in range(4):
        out_ref[x, :8, :] = update[8 * x : 8 * x + 8]
        out_ref[x, 8:, :] = own[8 * x : 8 * x + 8]


def chain(place, strips, halves):
    return pl.pallas_call(
        chain_kernel,
        out_shape=jax.ShapeDtypeStruct((4, 16, 2 * TILE), jnp.float32),
        in_specs=[SMEM, VMEM, VMEM],
        out_specs=VMEM,
        scratch_shapes=[pltpu.VMEM((PADDED, PADDED), jnp.bfloat16)] * 2
        + [pltpu.VMEM((PADDED, 2 * TILE), jnp.bfloat16)] * 3,
        compiler_params=pltpu.CompilerParams(vmem_limit_bytes=24 << 20),
    )(place, strips, halves)


def finish_kernel(got_ref, momentum_ref, update_ref, new_ref, update_half, sum_half):
    for half in range(2):
        columns = slice(half * TILE, (half + 1) * TILE)
        for m in range(MATS):
            rows = pl.ds(m, 6, stride=MATS)
            update_half[rows, :] = got_ref[m, 0:6, columns]
            sum_half[rows, :] = got_ref[m, 8:14, columns]
        momentum = momentum_ref[:, columns]
        update_ref[:, columns] = update_half[...]
        new_ref[:, columns] = 0.95 * momentum + (sum_half[...] - KAPPA * momentum)


def finish(got, momentum):
    shape = jax.ShapeDtypeStruct(momentum.shape, jnp.float32)
    return pl.pallas_call(
        finish_kernel,
        out_shape=(shape, shape),
        in_specs=[VMEM, VMEM],
        out_specs=(VMEM, VMEM),
        scratch_shapes=[pltpu.VMEM((24, TILE), jnp.float32)] * 2,
        compiler_params=pltpu.CompilerParams(vmem_limit_bytes=4 << 20),
    )(got, momentum)


def exchange(x, axis):
    return lax.all_to_all(x, axis, split_axis=0, concat_axis=0, tiled=True)


def spread(x, axis, count):
    return exchange(jnp.broadcast_to(x[None], (count, *x.shape)), axis)


def per_device(partials, momentum):
    w, v, x, c = (lax.axis_index(name) for name in ("w", "v", "x", "c"))
    z = 3 * w + v
    first_row = 48 * v + 12 * x + 6 * c
    strip = c * 12 + x * 3 + v
    place = jnp.stack([c, (z * 4 + x) * 2 + c, first_row, strip]).astype(jnp.int32)
    keep, send = split(place, partials[0], momentum)
    got = lax.ppermute(send, "c", [(0, 1), (1, 0)])
    near = jnp.sum(exchange(keep + got, ("x", "v")), axis=0)
    own = jnp.sum(exchange(near, "w"), axis=0)
    half = spread(own, ("x", "v"), 12).reshape(KV_ROWS, TILE)
    halves = lax.all_gather(half, "c", axis=0, tiled=False)
    mine = jnp.sum(spread(gram(place, halves), "y", 8), axis=0)
    strips = lax.all_gather(spread(mine, ("x", "v"), 12), "c", axis=0, tiled=True)
    done = chain(place, strips, halves)
    return finish(exchange(done, "w"), momentum)


def solution(mesh):
    fine = Mesh(mesh.devices.reshape(4, 3, 4, 2, 8), ("w", "v", "x", "c", "y"))
    rows = ("w", "v", "x", "c")
    return jax.shard_map(
        per_device,
        mesh=fine,
        in_specs=(P(rows, None, "y"), P(rows, "y")),
        out_specs=(P(rows, "y"), P(rows, "y")),
        check_vma=False,
    )
```

```python
import functools
import math

import jax
import jax.numpy as jnp
import numpy as np
from jax import lax
from jax.experimental import pallas as pl
from jax.experimental.pallas import tpu as pltpu
from jax.sharding import Mesh
from jax.sharding import PartitionSpec as P

D = 2048
KV_ROWS = 576
MATS = 4
PADDED = 640
TILE = 128

coef_a = 3.4445
coef_b = -4.775
coef_c = 2.0315

GAIN = 1.95
KAPPA = 0.9025 / 1.95

BLOCK = 64

STRIPS = [((0, 0), (8, 8))]
STRIPS += [
    ((i, 2 * j), (i, 2 * j + 1))
    for i in range(1, 9)
    for j in range(i // 2 + 1)
    if (i, j) != (8, 4)
]
STARTS = [next(n for n, (a, _) in enumerate(STRIPS) if a[0] == i) for i in range(9)]
PAIRS = [(i, j) for i in range(5) for j in range(i + 1)]

CHUNKS = 4
SEND_LIMIT = 54788096

VMEM = pl.BlockSpec(memory_space=pltpu.VMEM)
HBM = pl.BlockSpec(memory_space=pltpu.HBM)
SMEM = pl.BlockSpec(memory_space=pltpu.SMEM)
NT = (((1,), (1,)), ((), ()))
NN = (((1,), (0,)), ((), ()))


def sort_chunk(q, place_ref, raw, held, wide, out_ref, other):
    core, own = place_ref[0], place_ref[1] * 24
    chunk = raw.shape[0] // CHUNKS

    def put(columns):
        rows = slice(q * chunk, (q + 1) * chunk)
        wide[rows, :] = raw[rows, columns].astype(jnp.float32)

        @pl.when(own // chunk == q)
        def _():
            wide[pl.ds(pl.multiple_of(own, 8), 24), :] += KAPPA * held[:, columns]

    @pl.when((core == 0) != other)
    def _():
        put(slice(0, TILE))

    @pl.when((core == 1) != other)
    def _():
        put(slice(TILE, 2 * TILE))

    for m in range(MATS):
        rows = pl.ds(q * chunk + m, chunk // MATS, stride=MATS)
        groups = slice(q * 12 // CHUNKS, (q + 1) * 12 // CHUNKS)
        out_ref[groups, m] = wide[rows, :].reshape(-1, 48, TILE)


def send_kernel(place_ref, partial_ref, held, out_ref, raw, wide, sems):
    chunk = raw.shape[0] // CHUNKS
    copies = []
    for q in range(CHUNKS):
        rows = pl.ds(q * chunk, chunk)
        copies.append(pltpu.make_async_copy(partial_ref.at[rows], raw.at[rows], sems.at[q]))
    for copy in copies:
        copy.start()
    for q in range(CHUNKS):
        copies[q].wait()
        sort_chunk(q, place_ref, raw, held, wide, out_ref, True)


def keep_kernel(place_ref, raw, held, out_ref, wide):
    for q in range(CHUNKS):
        sort_chunk(q, place_ref, raw, held, wide, out_ref, False)


HALF = jax.ShapeDtypeStruct((12, MATS, 48, TILE), jnp.float32)
WIDE = pltpu.VMEM((MATS * KV_ROWS, TILE), jnp.float32)
COST = pl.CostEstimate(flops=1 << 20, bytes_accessed=3 << 20, transcendentals=0)


def to_send(place, partial, momentum):
    return pl.pallas_call(
        send_kernel,
        out_shape=HALF,
        in_specs=[SMEM, HBM, VMEM],
        out_specs=VMEM,
        scratch_shapes=[
            pltpu.VMEM((MATS * KV_ROWS, 2 * TILE), jnp.bfloat16),
            WIDE,
            pltpu.SemaphoreType.DMA((CHUNKS,)),
        ],
        compiler_params=pltpu.CompilerParams(vmem_limit_bytes=SEND_LIMIT),
        cost_estimate=COST,
    )(place, partial, momentum)


def to_keep(place, partial, momentum):
    return pl.pallas_call(
        keep_kernel,
        out_shape=HALF,
        in_specs=[SMEM, VMEM, VMEM],
        out_specs=VMEM,
        scratch_shapes=[WIDE],
        compiler_params=pltpu.CompilerParams(vmem_limit_bytes=16 << 20),
        cost_estimate=COST,
    )(place, partial, momentum)


def gram_kernel(place_ref, halves_ref, out_ref):
    strip = place_ref[3]
    i, start = jnp.int32(0), jnp.int32(0)
    for begin, step in zip(STARTS[1:], np.diff(STARTS)):
        past = strip >= begin
        i += past.astype(jnp.int32)
        start += jnp.where(past, int(step), 0)
    j = 2 * (strip - start)
    ends = strip == 0
    sides = [(i, j), (jnp.where(ends, 8, i), jnp.where(ends, 8, j + 1))]
    for side, pair in enumerate(sides):
        picks = [pl.ds(pl.multiple_of(k * BLOCK, BLOCK), BLOCK) for k in pair]
        left, right = (
            jnp.concatenate([halves_ref[0, rows, :], halves_ref[1, rows, :]], 1) for rows in picks
        )
        out_ref[:, side * BLOCK : (side + 1) * BLOCK] = lax.dot_general(
            left,
            right,
            NT,
            precision=lax.Precision.HIGHEST,
            preferred_element_type=jnp.float32,
        )


def gram(place, halves):
    return pl.pallas_call(
        gram_kernel,
        out_shape=jax.ShapeDtypeStruct((BLOCK, TILE), jnp.float32),
        in_specs=[SMEM, VMEM],
        out_specs=VMEM,
        compiler_params=pltpu.CompilerParams(vmem_limit_bytes=24 << 20),
    )(place, halves)


def three(x):
    top = x.astype(jnp.bfloat16)
    rest = x - top.astype(jnp.float32)
    middle = rest.astype(jnp.bfloat16)
    bottom = (rest - middle.astype(jnp.float32)).astype(jnp.bfloat16)
    return top, middle, bottom


def times(x, right):
    n = x.shape[0]
    parts = three(x)
    total = 0.0
    for at, ref in reversed(list(enumerate(right))):
        product = lax.dot_general(
            jnp.concatenate(parts[: 3 - at], 0),
            ref[...],
            NN,
            preferred_element_type=jnp.float32,
        )
        for k in reversed(range(3 - at)):
            total = total + product[k * n : (k + 1) * n]
    return total


def triangle(strips_ref):
    zero = jnp.zeros((BLOCK, BLOCK), jnp.float32)
    strip = {}
    for at, ((i, j), other) in enumerate(STRIPS[1:], 1):
        strip[i, j // 2] = strips_ref[at]
    ends = strips_ref[0]
    strip[0, 0] = jnp.concatenate([ends[:, :BLOCK], strip[1, 0][:, :BLOCK].T], 1)
    strip[8, 4] = jnp.concatenate([ends[:, BLOCK:], zero], 1)
    blank = jnp.concatenate([zero, zero], 1)
    return {
        (i, j): jnp.concatenate([strip[2 * i, j], strip.get((2 * i + 1, j), blank)], 0)
        for i, j in PAIRS
    }


def chain_kernel(place_ref, strips_ref, halves_ref, out_ref, g0, g1, t0, t1, t2):
    first_row = place_ref[2]
    blocks = triangle(strips_ref)
    row = lax.broadcasted_iota(jnp.int32, (TILE, TILE), 0)
    column = lax.broadcasted_iota(jnp.int32, (TILE, TILE), 1)
    diagonal = jnp.zeros((TILE, TILE), jnp.float32)
    for i in range(5):
        diagonal += jnp.where(row == column, blocks[i, i], 0.0)
    squares = jnp.sum(jnp.sum(diagonal, axis=0, keepdims=True), axis=1, keepdims=True)
    scale = GAIN / (GAIN * jnp.sqrt(squares) + 1e-07)
    for i, j in PAIRS:
        block = (blocks[i, j] * scale) * scale
        here = (slice(i * TILE, (i + 1) * TILE), slice(j * TILE, (j + 1) * TILE))
        for ref, part in zip((g0, g1), three(block)):
            ref[here] = part
        if i != j:
            for ref, part in zip((g0, g1), three(block.T)):
                ref[here[1], here[0]] = part
    for half in range(2):
        for ref, part in zip((t0, t1, t2), three(halves_ref[half])):
            ref[:KV_ROWS, half * TILE : (half + 1) * TILE] = part
    for ref in (t0, t1, t2):
        ref[KV_ROWS:, :] = jnp.zeros((PADDED - KV_ROWS, 2 * TILE), jnp.bfloat16)
    g, t = (g0, g1), (t0, t1, t2)

    r = lax.broadcasted_iota(jnp.int32, (32, PADDED), 0)
    k = lax.broadcasted_iota(jnp.int32, (32, PADDED), 1)
    wanted = first_row + 144 * (r >> 3) + (r & 7)
    pick = jnp.where(jnp.logical_and(k == wanted, (r & 7) < 6), 1.0, 0.0)

    def poly(x):
        once = times(x, g)
        return coef_a * x + coef_b * once + coef_c * times(once, g)

    first = poly(pick)
    second = times(poly(poly(first)), g)
    third = times(poly(poly(second)), g)
    rows = coef_a * first + coef_b * second + coef_c * third
    gain = (0.2 * math.sqrt(max(KV_ROWS, D))) * scale
    both = times(jnp.concatenate([rows, pick], 0), t)
    update, own = gain * both[:32], both[32:]
    for x in range(4):
        out_ref[x, :8, :] = update[8 * x : 8 * x + 8]
        out_ref[x, 8:, :] = own[8 * x : 8 * x + 8]


def chain(place, strips, halves):
    return pl.pallas_call(
        chain_kernel,
        out_shape=jax.ShapeDtypeStruct((4, 16, 2 * TILE), jnp.float32),
        in_specs=[SMEM, VMEM, VMEM],
        out_specs=VMEM,
        scratch_shapes=[pltpu.VMEM((PADDED, PADDED), jnp.bfloat16)] * 2
        + [pltpu.VMEM((PADDED, 2 * TILE), jnp.bfloat16)] * 3,
        compiler_params=pltpu.CompilerParams(vmem_limit_bytes=24 << 20),
    )(place, strips, halves)


def finish_kernel(got_ref, momentum_ref, update_ref, new_ref, update_half, sum_half):
    for half in range(2):
        columns = slice(half * TILE, (half + 1) * TILE)
        for m in range(MATS):
            rows = pl.ds(m, 6, stride=MATS)
            update_half[rows, :] = got_ref[m, 0:6, columns]
            sum_half[rows, :] = got_ref[m, 8:14, columns]
        momentum = momentum_ref[:, columns]
        update_ref[:, columns] = update_half[...]
        new_ref[:, columns] = 0.95 * momentum + (sum_half[...] - KAPPA * momentum)


def finish(got, momentum):
    shape = jax.ShapeDtypeStruct(momentum.shape, jnp.float32)
    return pl.pallas_call(
        finish_kernel,
        out_shape=(shape, shape),
        in_specs=[VMEM, VMEM],
        out_specs=(VMEM, VMEM),
        scratch_shapes=[pltpu.VMEM((24, TILE), jnp.float32)] * 2,
        compiler_params=pltpu.CompilerParams(vmem_limit_bytes=4 << 20),
    )(got, momentum)


def exchange(x, axis):
    return lax.all_to_all(x, axis, split_axis=0, concat_axis=0, tiled=True)


def spread(x, axis, count):
    return exchange(jnp.broadcast_to(x[None], (count, *x.shape)), axis)


def per_device(partials, momentum):
    w, v, x, c = (lax.axis_index(name) for name in ("w", "v", "x", "c"))
    z = 3 * w + v
    first_row = 48 * v + 12 * x + 6 * c
    strip = c * 12 + v * 4 + x
    place = jnp.stack([c, (z * 4 + x) * 2 + c, first_row, strip]).astype(jnp.int32)
    send = to_send(place, partials[0], momentum)
    got = lax.ppermute(send, "c", [(0, 1), (1, 0)])
    keep = to_keep(place, partials[0], momentum)
    near = jnp.sum(exchange(keep + got, ("v", "x")), axis=0)
    own = jnp.sum(exchange(near, "w"), axis=0)
    half = spread(own, ("v", "x"), 12).reshape(KV_ROWS, TILE)
    halves = lax.all_gather(half, "c", axis=0, tiled=False)
    mine = jnp.sum(spread(gram(place, halves), "y", 8), axis=0)
    strips = lax.all_gather(spread(mine, ("v", "x"), 12), "c", axis=0, tiled=True)
    done = chain(place, strips, halves)
    return finish(exchange(done, "w"), momentum)


def solution(mesh):
    fine = Mesh(mesh.devices.reshape(4, 3, 4, 2, 8), ("w", "v", "x", "c", "y"))
    rows = ("w", "v", "x", "c")
    return jax.shard_map(
        per_device,
        mesh=fine,
        in_specs=(P(rows, None, "y"), P(rows, "y")),
        out_specs=(P(rows, "y"), P(rows, "y")),
        check_vma=False,
    )
```

```python
import functools
import math

import jax
import jax.numpy as jnp
import numpy as np
from jax import lax
from jax.experimental import pallas as pl
from jax.experimental.pallas import tpu as pltpu
from jax.sharding import Mesh
from jax.sharding import PartitionSpec as P

D = 2048
KV_ROWS = 576
MATS = 4
PADDED = 640
TILE = 128

coef_a = 3.4445
coef_b = -4.775
coef_c = 2.0315

GAIN = 1.95
KAPPA = 0.9025 / 1.95

BLOCK = 64

STRIPS = [((0, 0), (8, 8))]
STRIPS += [
    ((i, 2 * j), (i, 2 * j + 1))
    for i in range(1, 9)
    for j in range(i // 2 + 1)
    if (i, j) != (8, 4)
]
STARTS = [next(n for n, (a, _) in enumerate(STRIPS) if a[0] == i) for i in range(9)]
PAIRS = [(i, j) for i in range(5) for j in range(i + 1)]

CHUNKS = 4
SEND_LIMIT = 54788096

VMEM = pl.BlockSpec(memory_space=pltpu.VMEM)
HBM = pl.BlockSpec(memory_space=pltpu.HBM)
SMEM = pl.BlockSpec(memory_space=pltpu.SMEM)
NT = (((1,), (1,)), ((), ()))
NN = (((1,), (0,)), ((), ()))


def sort_chunk(q, place_ref, raw, held, wide, out_ref, other):
    core, own = place_ref[0], place_ref[1] * 24
    chunk = raw.shape[0] // CHUNKS

    def put(columns):
        rows = slice(q * chunk, (q + 1) * chunk)
        wide[rows, :] = raw[rows, columns].astype(jnp.float32)

        @pl.when(own // chunk == q)
        def _():
            wide[pl.ds(pl.multiple_of(own, 8), 24), :] += KAPPA * held[:, columns]

    @pl.when((core == 0) != other)
    def _():
        put(slice(0, TILE))

    @pl.when((core == 1) != other)
    def _():
        put(slice(TILE, 2 * TILE))

    for n in range(q * 12 // CHUNKS, (q + 1) * 12 // CHUNKS):
        for m in range(MATS):
            out_ref[n % 3 * 4 + n // 3, m] = wide[pl.ds(n * 192 + m, 48, stride=MATS), :]


def send_kernel(place_ref, partial_ref, held, out_ref, raw, wide, sems):
    chunk = raw.shape[0] // CHUNKS
    copies = []
    for q in range(CHUNKS):
        rows = pl.ds(q * chunk, chunk)
        copies.append(pltpu.make_async_copy(partial_ref.at[rows], raw.at[rows], sems.at[q]))
    for copy in copies:
        copy.start()
    for q in range(CHUNKS):
        copies[q].wait()
        sort_chunk(q, place_ref, raw, held, wide, out_ref, True)


def keep_kernel(place_ref, raw, held, out_ref, wide):
    for q in range(CHUNKS):
        sort_chunk(q, place_ref, raw, held, wide, out_ref, False)


HALF = jax.ShapeDtypeStruct((12, MATS, 48, TILE), jnp.float32)
WIDE = pltpu.VMEM((MATS * KV_ROWS, TILE), jnp.float32)
COST = pl.CostEstimate(flops=1 << 20, bytes_accessed=3 << 20, transcendentals=0)


def to_send(place, partial, momentum):
    return pl.pallas_call(
        send_kernel,
        out_shape=HALF,
        in_specs=[SMEM, HBM, VMEM],
        out_specs=VMEM,
        scratch_shapes=[
            pltpu.VMEM((MATS * KV_ROWS, 2 * TILE), jnp.bfloat16),
            WIDE,
            pltpu.SemaphoreType.DMA((CHUNKS,)),
        ],
        compiler_params=pltpu.CompilerParams(vmem_limit_bytes=SEND_LIMIT),
        cost_estimate=COST,
    )(place, partial, momentum)


def to_keep(place, partial, momentum):
    return pl.pallas_call(
        keep_kernel,
        out_shape=HALF,
        in_specs=[SMEM, VMEM, VMEM],
        out_specs=VMEM,
        scratch_shapes=[WIDE],
        compiler_params=pltpu.CompilerParams(vmem_limit_bytes=16 << 20),
        cost_estimate=COST,
    )(place, partial, momentum)


def gram_kernel(place_ref, halves_ref, out_ref):
    strip = place_ref[3]
    i, start = jnp.int32(0), jnp.int32(0)
    for begin, step in zip(STARTS[1:], np.diff(STARTS)):
        past = strip >= begin
        i += past.astype(jnp.int32)
        start += jnp.where(past, int(step), 0)
    j = 2 * (strip - start)
    ends = strip == 0
    sides = [(i, j), (jnp.where(ends, 8, i), jnp.where(ends, 8, j + 1))]
    for side, pair in enumerate(sides):
        picks = [pl.ds(pl.multiple_of(k * BLOCK, BLOCK), BLOCK) for k in pair]
        left, right = (
            jnp.concatenate([halves_ref[0, rows, :], halves_ref[1, rows, :]], 1) for rows in picks
        )
        out_ref[:, side * BLOCK : (side + 1) * BLOCK] = lax.dot_general(
            left,
            right,
            NT,
            precision=lax.Precision.HIGHEST,
            preferred_element_type=jnp.float32,
        )


def gram(place, halves):
    return pl.pallas_call(
        gram_kernel,
        out_shape=jax.ShapeDtypeStruct((BLOCK, TILE), jnp.float32),
        in_specs=[SMEM, VMEM],
        out_specs=VMEM,
        compiler_params=pltpu.CompilerParams(vmem_limit_bytes=24 << 20),
    )(place, halves)


def three(x):
    top = x.astype(jnp.bfloat16)
    rest = x - top.astype(jnp.float32)
    middle = rest.astype(jnp.bfloat16)
    bottom = (rest - middle.astype(jnp.float32)).astype(jnp.bfloat16)
    return top, middle, bottom


def times(x, right):
    n = x.shape[0]
    parts = three(x)
    total = 0.0
    for at, ref in reversed(list(enumerate(right))):
        product = lax.dot_general(
            jnp.concatenate(parts[: 3 - at], 0),
            ref[...],
            NN,
            preferred_element_type=jnp.float32,
        )
        for k in reversed(range(3 - at)):
            total = total + product[k * n : (k + 1) * n]
    return total


def triangle(strips_ref):
    zero = jnp.zeros((BLOCK, BLOCK), jnp.float32)
    strip = {}
    for at, ((i, j), other) in enumerate(STRIPS[1:], 1):
        strip[i, j // 2] = strips_ref[at]
    ends = strips_ref[0]
    strip[0, 0] = jnp.concatenate([ends[:, :BLOCK], strip[1, 0][:, :BLOCK].T], 1)
    strip[8, 4] = jnp.concatenate([ends[:, BLOCK:], zero], 1)
    blank = jnp.concatenate([zero, zero], 1)
    return {
        (i, j): jnp.concatenate([strip[2 * i, j], strip.get((2 * i + 1, j), blank)], 0)
        for i, j in PAIRS
    }


def chain_kernel(place_ref, strips_ref, halves_ref, out_ref, g0, g1, t0, t1, t2):
    first_row = place_ref[2]
    blocks = triangle(strips_ref)
    row = lax.broadcasted_iota(jnp.int32, (TILE, TILE), 0)
    column = lax.broadcasted_iota(jnp.int32, (TILE, TILE), 1)
    diagonal = jnp.zeros((TILE, TILE), jnp.float32)
    for i in range(5):
        diagonal += jnp.where(row == column, blocks[i, i], 0.0)
    squares = jnp.sum(jnp.sum(diagonal, axis=0, keepdims=True), axis=1, keepdims=True)
    scale = GAIN / (GAIN * jnp.sqrt(squares) + 1e-07)
    for i, j in PAIRS:
        block = (blocks[i, j] * scale) * scale
        here = (slice(i * TILE, (i + 1) * TILE), slice(j * TILE, (j + 1) * TILE))
        for ref, part in zip((g0, g1), three(block)):
            ref[here] = part
        if i != j:
            for ref, part in zip((g0, g1), three(block.T)):
                ref[here[1], here[0]] = part
    for half in range(2):
        for ref, part in zip((t0, t1, t2), three(halves_ref[half])):
            ref[:KV_ROWS, half * TILE : (half + 1) * TILE] = part
    for ref in (t0, t1, t2):
        ref[KV_ROWS:, :] = jnp.zeros((PADDED - KV_ROWS, 2 * TILE), jnp.bfloat16)
    g, t = (g0, g1), (t0, t1, t2)

    r = lax.broadcasted_iota(jnp.int32, (32, PADDED), 0)
    k = lax.broadcasted_iota(jnp.int32, (32, PADDED), 1)
    wanted = first_row + 144 * (r >> 3) + (r & 7)
    pick = jnp.where(jnp.logical_and(k == wanted, (r & 7) < 6), 1.0, 0.0)

    def poly(x):
        once = times(x, g)
        return coef_a * x + coef_b * once + coef_c * times(once, g)

    first = poly(pick)
    second = times(poly(poly(first)), g)
    third = times(poly(poly(second)), g)
    rows = coef_a * first + coef_b * second + coef_c * third
    gain = (0.2 * math.sqrt(max(KV_ROWS, D))) * scale
    both = times(jnp.concatenate([rows, pick], 0), t)
    update, own = gain * both[:32], both[32:]
    for x in range(4):
        out_ref[x, :8, :] = update[8 * x : 8 * x + 8]
        out_ref[x, 8:, :] = own[8 * x : 8 * x + 8]


def chain(place, strips, halves):
    return pl.pallas_call(
        chain_kernel,
        out_shape=jax.ShapeDtypeStruct((4, 16, 2 * TILE), jnp.float32),
        in_specs=[SMEM, VMEM, VMEM],
        out_specs=VMEM,
        scratch_shapes=[pltpu.VMEM((PADDED, PADDED), jnp.bfloat16)] * 2
        + [pltpu.VMEM((PADDED, 2 * TILE), jnp.bfloat16)] * 3,
        compiler_params=pltpu.CompilerParams(vmem_limit_bytes=24 << 20),
    )(place, strips, halves)


def finish_kernel(got_ref, momentum_ref, update_ref, new_ref, update_half, sum_half):
    for half in range(2):
        columns = slice(half * TILE, (half + 1) * TILE)
        for m in range(MATS):
            rows = pl.ds(m, 6, stride=MATS)
            update_half[rows, :] = got_ref[m, 0:6, columns]
            sum_half[rows, :] = got_ref[m, 8:14, columns]
        momentum = momentum_ref[:, columns]
        update_ref[:, columns] = update_half[...]
        new_ref[:, columns] = 0.95 * momentum + (sum_half[...] - KAPPA * momentum)


def finish(got, momentum):
    shape = jax.ShapeDtypeStruct(momentum.shape, jnp.float32)
    return pl.pallas_call(
        finish_kernel,
        out_shape=(shape, shape),
        in_specs=[VMEM, VMEM],
        out_specs=(VMEM, VMEM),
        scratch_shapes=[pltpu.VMEM((24, TILE), jnp.float32)] * 2,
        compiler_params=pltpu.CompilerParams(vmem_limit_bytes=4 << 20),
    )(got, momentum)


def exchange(x, axis):
    return lax.all_to_all(x, axis, split_axis=0, concat_axis=0, tiled=True)


def spread(x, axis, count):
    return exchange(jnp.broadcast_to(x[None], (count, *x.shape)), axis)


def per_device(partials, momentum):
    w, v, x, c = (lax.axis_index(name) for name in ("w", "v", "x", "c"))
    z = 3 * w + v
    first_row = 48 * v + 12 * x + 6 * c
    strip = c * 12 + v * 4 + x
    place = jnp.stack([c, (z * 4 + x) * 2 + c, first_row, strip]).astype(jnp.int32)
    send = to_send(place, partials[0], momentum)
    got = lax.ppermute(send, "c", [(0, 1), (1, 0)])
    keep = to_keep(place, partials[0], momentum)
    near = jnp.sum(exchange(keep + got, ("v", "x")), axis=0)
    own = jnp.sum(exchange(near, "w"), axis=0)
    half = spread(own, ("x", "v"), 12).reshape(KV_ROWS, TILE)
    halves = lax.all_gather(half, "c", axis=0, tiled=False)
    mine = jnp.sum(spread(gram(place, halves), "y", 8), axis=0)
    strips = lax.all_gather(spread(mine, ("v", "x"), 12), "c", axis=0, tiled=True)
    done = chain(place, strips, halves)
    return finish(exchange(done, "w"), momentum)


def solution(mesh):
    fine = Mesh(mesh.devices.reshape(4, 3, 4, 2, 8), ("w", "v", "x", "c", "y"))
    rows = ("w", "v", "x", "c")
    return jax.shard_map(
        per_device,
        mesh=fine,
        in_specs=(P(rows, None, "y"), P(rows, "y")),
        out_specs=(P(rows, "y"), P(rows, "y")),
        check_vma=False,
    )
```

```python
import functools
import math

import jax
import jax.numpy as jnp
import numpy as np
from jax import lax
from jax.experimental import pallas as pl
from jax.experimental.pallas import tpu as pltpu
from jax.sharding import Mesh
from jax.sharding import PartitionSpec as P

D = 2048
KV_ROWS = 576
MATS = 4
PADDED = 640
TILE = 128

coef_a = 3.4445
coef_b = -4.775
coef_c = 2.0315

GAIN = 1.95
KAPPA = 0.9025 / 1.95

BLOCK = 64

STRIPS = [((0, 0), (8, 8))]
STRIPS += [
    ((i, 2 * j), (i, 2 * j + 1))
    for i in range(1, 9)
    for j in range(i // 2 + 1)
    if (i, j) != (8, 4)
]
STARTS = [next(n for n, (a, _) in enumerate(STRIPS) if a[0] == i) for i in range(9)]
PAIRS = [(i, j) for i in range(5) for j in range(i + 1)]

CHUNKS = 4
SEND_LIMIT = 54788096

VMEM = pl.BlockSpec(memory_space=pltpu.VMEM)
HBM = pl.BlockSpec(memory_space=pltpu.HBM)
SMEM = pl.BlockSpec(memory_space=pltpu.SMEM)
NT = (((1,), (1,)), ((), ()))
NN = (((1,), (0,)), ((), ()))


def sort_chunk(q, place_ref, raw, held, wide, out_ref, other):
    core, own = place_ref[0], place_ref[1] * 24
    chunk = raw.shape[0] // CHUNKS

    def put(columns):
        rows = slice(q * chunk, (q + 1) * chunk)
        wide[rows, :] = raw[rows, columns].astype(jnp.float32)

        @pl.when(own // chunk == q)
        def _():
            wide[pl.ds(pl.multiple_of(own, 8), 24), :] += KAPPA * held[:, columns]

    @pl.when((core == 0) != other)
    def _():
        put(slice(0, TILE))

    @pl.when((core == 1) != other)
    def _():
        put(slice(TILE, 2 * TILE))

    for n in range(q * 12 // CHUNKS, (q + 1) * 12 // CHUNKS):
        for m in range(MATS):
            out_ref[n % 3 * 4 + n // 3, m] = wide[pl.ds(n * 192 + m, 48, stride=MATS), :]


def send_kernel(place_ref, partial_ref, held, out_ref, raw, wide, sems):
    chunk = raw.shape[0] // CHUNKS
    copies = []
    for q in range(CHUNKS):
        rows = pl.ds(q * chunk, chunk)
        copies.append(pltpu.make_async_copy(partial_ref.at[rows], raw.at[rows], sems.at[q]))
    for copy in copies:
        copy.start()
    for q in range(CHUNKS):
        copies[q].wait()
        sort_chunk(q, place_ref, raw, held, wide, out_ref, True)


def keep_kernel(place_ref, raw, held, out_ref, wide):
    for q in range(CHUNKS):
        sort_chunk(q, place_ref, raw, held, wide, out_ref, False)


HALF = jax.ShapeDtypeStruct((12, MATS, 48, TILE), jnp.float32)
WIDE = pltpu.VMEM((MATS * KV_ROWS, TILE), jnp.float32)
COST = pl.CostEstimate(flops=1 << 20, bytes_accessed=3 << 20, transcendentals=0)


def to_send(place, partial, momentum):
    return pl.pallas_call(
        send_kernel,
        out_shape=HALF,
        in_specs=[SMEM, HBM, VMEM],
        out_specs=VMEM,
        scratch_shapes=[
            pltpu.VMEM((MATS * KV_ROWS, 2 * TILE), jnp.bfloat16),
            WIDE,
            pltpu.SemaphoreType.DMA((CHUNKS,)),
        ],
        compiler_params=pltpu.CompilerParams(vmem_limit_bytes=SEND_LIMIT),
        cost_estimate=COST,
    )(place, partial, momentum)


def to_keep(place, partial, momentum):
    return pl.pallas_call(
        keep_kernel,
        out_shape=HALF,
        in_specs=[SMEM, VMEM, VMEM],
        out_specs=VMEM,
        scratch_shapes=[WIDE],
        compiler_params=pltpu.CompilerParams(vmem_limit_bytes=16 << 20),
        cost_estimate=COST,
    )(place, partial, momentum)


def gram_kernel(place_ref, halves_ref, out_ref):
    strip = place_ref[3]
    i, start = jnp.int32(0), jnp.int32(0)
    for begin, step in zip(STARTS[1:], np.diff(STARTS)):
        past = strip >= begin
        i += past.astype(jnp.int32)
        start += jnp.where(past, int(step), 0)
    j = 2 * (strip - start)
    ends = strip == 0
    sides = [(i, j), (jnp.where(ends, 8, i), jnp.where(ends, 8, j + 1))]
    for side, pair in enumerate(sides):
        picks = [pl.ds(pl.multiple_of(k * BLOCK, BLOCK), BLOCK) for k in pair]
        left, right = (
            jnp.concatenate([halves_ref[0, rows, :], halves_ref[1, rows, :]], 1) for rows in picks
        )
        out_ref[:, side * BLOCK : (side + 1) * BLOCK] = lax.dot_general(
            left,
            right,
            NT,
            precision=lax.Precision.HIGHEST,
            preferred_element_type=jnp.float32,
        )


def gram(place, halves):
    return pl.pallas_call(
        gram_kernel,
        out_shape=jax.ShapeDtypeStruct((BLOCK, TILE), jnp.float32),
        in_specs=[SMEM, VMEM],
        out_specs=VMEM,
        compiler_params=pltpu.CompilerParams(vmem_limit_bytes=24 << 20),
    )(place, halves)


def three(x):
    top = x.astype(jnp.bfloat16)
    rest = x - top.astype(jnp.float32)
    middle = rest.astype(jnp.bfloat16)
    bottom = (rest - middle.astype(jnp.float32)).astype(jnp.bfloat16)
    return top, middle, bottom


def times(x, right):
    n = x.shape[0]
    parts = three(x)
    total = 0.0
    for at, ref in reversed(list(enumerate(right))):
        product = lax.dot_general(
            jnp.concatenate(parts[: 3 - at], 0),
            ref[...],
            NN,
            preferred_element_type=jnp.float32,
        )
        for k in reversed(range(3 - at)):
            total = total + product[k * n : (k + 1) * n]
    return total


def triangle(strips_ref):
    zero = jnp.zeros((BLOCK, BLOCK), jnp.float32)
    strip = {}
    for at, ((i, j), other) in enumerate(STRIPS[1:], 1):
        strip[i, j // 2] = strips_ref[at]
    ends = strips_ref[0]
    strip[0, 0] = jnp.concatenate([ends[:, :BLOCK], strip[1, 0][:, :BLOCK].T], 1)
    strip[8, 4] = jnp.concatenate([ends[:, BLOCK:], zero], 1)
    blank = jnp.concatenate([zero, zero], 1)
    return {
        (i, j): jnp.concatenate([strip[2 * i, j], strip.get((2 * i + 1, j), blank)], 0)
        for i, j in PAIRS
    }


def chain_kernel(place_ref, strips_ref, halves_ref, out_ref, g0, g1, t0, t1, t2):
    first_row = place_ref[2]
    blocks = triangle(strips_ref)
    row = lax.broadcasted_iota(jnp.int32, (TILE, TILE), 0)
    column = lax.broadcasted_iota(jnp.int32, (TILE, TILE), 1)
    diagonal = jnp.zeros((TILE, TILE), jnp.float32)
    for i in range(5):
        diagonal += jnp.where(row == column, blocks[i, i], 0.0)
    squares = jnp.sum(jnp.sum(diagonal, axis=0, keepdims=True), axis=1, keepdims=True)
    scale = GAIN / (GAIN * jnp.sqrt(squares) + 1e-07)
    for i, j in PAIRS:
        block = (blocks[i, j] * scale) * scale
        here = (slice(i * TILE, (i + 1) * TILE), slice(j * TILE, (j + 1) * TILE))
        for ref, part in zip((g0, g1), three(block)):
            ref[here] = part
        if i != j:
            for ref, part in zip((g0, g1), three(block.T)):
                ref[here[1], here[0]] = part
    for half in range(2):
        for ref, part in zip((t0, t1, t2), three(halves_ref[half])):
            ref[:KV_ROWS, half * TILE : (half + 1) * TILE] = part
    for ref in (t0, t1, t2):
        ref[KV_ROWS:, :] = jnp.zeros((PADDED - KV_ROWS, 2 * TILE), jnp.bfloat16)
    g, t = (g0, g1), (t0, t1, t2)

    r = lax.broadcasted_iota(jnp.int32, (32, PADDED), 0)
    k = lax.broadcasted_iota(jnp.int32, (32, PADDED), 1)
    wanted = first_row + 144 * (r >> 3) + (r & 7)
    pick = jnp.where(jnp.logical_and(k == wanted, (r & 7) < 6), 1.0, 0.0)

    def poly(x):
        once = times(x, g)
        return coef_a * x + coef_b * once + coef_c * times(once, g)

    first = poly(pick)
    second = times(poly(poly(first)), g)
    third = times(poly(poly(second)), g)
    rows = coef_a * first + coef_b * second + coef_c * third
    gain = (0.2 * math.sqrt(max(KV_ROWS, D))) * scale
    both = times(jnp.concatenate([rows, pick], 0), t)
    update, own = gain * both[:32], both[32:]
    for x in range(4):
        out_ref[x, :8, :] = update[8 * x : 8 * x + 8]
        out_ref[x, 8:, :] = own[8 * x : 8 * x + 8]


def chain(place, strips, halves):
    return pl.pallas_call(
        chain_kernel,
        out_shape=jax.ShapeDtypeStruct((4, 16, 2 * TILE), jnp.float32),
        in_specs=[SMEM, VMEM, VMEM],
        out_specs=VMEM,
        scratch_shapes=[pltpu.VMEM((PADDED, PADDED), jnp.bfloat16)] * 2
        + [pltpu.VMEM((PADDED, 2 * TILE), jnp.bfloat16)] * 3,
        compiler_params=pltpu.CompilerParams(vmem_limit_bytes=24 << 20),
    )(place, strips, halves)


def finish_kernel(got_ref, momentum_ref, update_ref, new_ref, update_half, sum_half):
    for half in range(2):
        columns = slice(half * TILE, (half + 1) * TILE)
        for m in range(MATS):
            rows = pl.ds(m, 6, stride=MATS)
            update_half[rows, :] = got_ref[m, 0:6, columns]
            sum_half[rows, :] = got_ref[m, 8:14, columns]
        momentum = momentum_ref[:, columns]
        update_ref[:, columns] = update_half[...]
        new_ref[:, columns] = 0.95 * momentum + (sum_half[...] - KAPPA * momentum)


def finish(got, momentum):
    shape = jax.ShapeDtypeStruct(momentum.shape, jnp.float32)
    return pl.pallas_call(
        finish_kernel,
        out_shape=(shape, shape),
        in_specs=[VMEM, VMEM],
        out_specs=(VMEM, VMEM),
        scratch_shapes=[pltpu.VMEM((24, TILE), jnp.float32)] * 2,
        compiler_params=pltpu.CompilerParams(vmem_limit_bytes=4 << 20),
    )(got, momentum)


def exchange(x, axis):
    return lax.all_to_all(x, axis, split_axis=0, concat_axis=0, tiled=True)


def spread(x, axis, count):
    return exchange(jnp.broadcast_to(x[None], (count, *x.shape)), axis)


def per_device(partials, momentum):
    w, v, x, c = (lax.axis_index(name) for name in ("w", "v", "x", "c"))
    z = 3 * w + v
    first_row = 48 * v + 12 * x + 6 * c
    strip = c * 12 + v * 4 + x
    place = jnp.stack([c, (z * 4 + x) * 2 + c, first_row, strip]).astype(jnp.int32)
    send = to_send(place, partials[0], momentum)
    got = lax.ppermute(send, "c", [(0, 1), (1, 0)])
    keep = to_keep(place, partials[0], momentum)
    near = jnp.sum(exchange(keep + got, ("v", "x")), axis=0)
    thrice = jnp.broadcast_to(near[:, None], (MATS, 3, 48, TILE)).reshape(12, 48, TILE)
    by_z = exchange(thrice, ("w", "v")).reshape(4, 3, 48, TILE)
    own = jnp.sum(by_z, axis=0).reshape(144, TILE)
    half = spread(own, "x", 4).reshape(KV_ROWS, TILE)
    halves = lax.all_gather(half, "c", axis=0, tiled=False)
    mine = jnp.sum(spread(gram(place, halves), "y", 8), axis=0)
    strips = lax.all_gather(spread(mine, ("v", "x"), 12), "c", axis=0, tiled=True)
    done = chain(place, strips, halves)
    return finish(exchange(done, "w"), momentum)


def solution(mesh):
    fine = Mesh(mesh.devices.reshape(4, 3, 4, 2, 8), ("w", "v", "x", "c", "y"))
    rows = ("w", "v", "x", "c")
    return jax.shard_map(
        per_device,
        mesh=fine,
        in_specs=(P(rows, None, "y"), P(rows, "y")),
        out_specs=(P(rows, "y"), P(rows, "y")),
        check_vma=False,
    )
```

```python
import functools
import math

import jax
import jax.numpy as jnp
import numpy as np
from jax import lax
from jax.experimental import pallas as pl
from jax.experimental.pallas import tpu as pltpu
from jax.sharding import Mesh
from jax.sharding import PartitionSpec as P

D = 2048
KV_ROWS = 576
MATS = 4
PADDED = 640
TILE = 128

coef_a = 3.4445
coef_b = -4.775
coef_c = 2.0315

GAIN = 1.95
KAPPA = 0.9025 / 1.95

BLOCK = 64

STRIPS = [((0, 0), (8, 8))]
STRIPS += [
    ((i, 2 * j), (i, 2 * j + 1))
    for i in range(1, 9)
    for j in range(i // 2 + 1)
    if (i, j) != (8, 4)
]
STARTS = [next(n for n, (a, _) in enumerate(STRIPS) if a[0] == i) for i in range(9)]
PAIRS = [(i, j) for i in range(5) for j in range(i + 1)]

CHUNKS = 4
SEND_LIMIT = 54788096

VMEM = pl.BlockSpec(memory_space=pltpu.VMEM)
HBM = pl.BlockSpec(memory_space=pltpu.HBM)
SMEM = pl.BlockSpec(memory_space=pltpu.SMEM)
NT = (((1,), (1,)), ((), ()))
NN = (((1,), (0,)), ((), ()))


def sort_chunk(q, first, own_rows, wide, out_ref):
    chunk = wide.shape[0] // CHUNKS

    @pl.when(first // chunk == q)
    def _():
        wide[pl.ds(pl.multiple_of(first, 8), 24), :] += KAPPA * own_rows

    for m in range(MATS):
        rows = pl.ds(q * chunk + m, chunk // MATS, stride=MATS)
        groups = slice(q * 12 // CHUNKS, (q + 1) * 12 // CHUNKS)
        out_ref[groups, m] = wide[rows, :].reshape(-1, 48, TILE)


def send_kernel(place_ref, partial_ref, held, out_ref, raw, wide, sems):
    core, first = place_ref[0], place_ref[1] * 24
    chunk = raw.shape[0] // CHUNKS
    columns = pl.ds(pl.multiple_of((1 - core) * TILE, TILE), TILE)
    copies = []
    for q in range(CHUNKS):
        rows = pl.ds(q * chunk, chunk)
        copies.append(
            pltpu.make_async_copy(partial_ref.at[rows, columns], raw.at[rows], sems.at[q])
        )
    for copy in copies:
        copy.start()
    own_rows = held[:, columns]
    for q in range(CHUNKS):
        copies[q].wait()
        rows = slice(q * chunk, (q + 1) * chunk)
        wide[rows, :] = raw[rows, :].astype(jnp.float32)
        sort_chunk(q, first, own_rows, wide, out_ref)


def keep_kernel(place_ref, raw, held, out_ref, wide):
    core, first = place_ref[0], place_ref[1] * 24
    chunk = raw.shape[0] // CHUNKS
    columns = pl.ds(pl.multiple_of(core * TILE, TILE), TILE)
    own_rows = held[:, columns]
    for q in range(CHUNKS):
        rows = slice(q * chunk, (q + 1) * chunk)
        wide[rows, :] = raw[rows, columns].astype(jnp.float32)
        sort_chunk(q, first, own_rows, wide, out_ref)


HALF = jax.ShapeDtypeStruct((12, MATS, 48, TILE), jnp.float32)
WIDE = pltpu.VMEM((MATS * KV_ROWS, TILE), jnp.float32)
COST = pl.CostEstimate(flops=1 << 20, bytes_accessed=3 << 20, transcendentals=0)


def to_send(place, partial, momentum):
    return pl.pallas_call(
        send_kernel,
        out_shape=HALF,
        in_specs=[SMEM, HBM, VMEM],
        out_specs=VMEM,
        scratch_shapes=[
            pltpu.VMEM((MATS * KV_ROWS, TILE), jnp.bfloat16),
            WIDE,
            pltpu.SemaphoreType.DMA((CHUNKS,)),
        ],
        compiler_params=pltpu.CompilerParams(vmem_limit_bytes=SEND_LIMIT),
        cost_estimate=COST,
    )(place, partial, momentum)


def to_keep(place, partial, momentum):
    return pl.pallas_call(
        keep_kernel,
        out_shape=HALF,
        in_specs=[SMEM, VMEM, VMEM],
        out_specs=VMEM,
        scratch_shapes=[WIDE],
        compiler_params=pltpu.CompilerParams(vmem_limit_bytes=16 << 20),
        cost_estimate=COST,
    )(place, partial, momentum)


def gram_kernel(place_ref, halves_ref, out_ref):
    strip = place_ref[3]
    i, start = jnp.int32(0), jnp.int32(0)
    for begin, step in zip(STARTS[1:], np.diff(STARTS)):
        past = strip >= begin
        i += past.astype(jnp.int32)
        start += jnp.where(past, int(step), 0)
    j = 2 * (strip - start)
    ends = strip == 0
    sides = [(i, j), (jnp.where(ends, 8, i), jnp.where(ends, 8, j + 1))]
    for side, pair in enumerate(sides):
        picks = [pl.ds(pl.multiple_of(k * BLOCK, BLOCK), BLOCK) for k in pair]
        left, right = (
            jnp.concatenate([halves_ref[0, rows, :], halves_ref[1, rows, :]], 1) for rows in picks
        )
        out_ref[:, side * BLOCK : (side + 1) * BLOCK] = lax.dot_general(
            left,
            right,
            NT,
            precision=lax.Precision.HIGHEST,
            preferred_element_type=jnp.float32,
        )


def gram(place, halves):
    return pl.pallas_call(
        gram_kernel,
        out_shape=jax.ShapeDtypeStruct((BLOCK, TILE), jnp.float32),
        in_specs=[SMEM, VMEM],
        out_specs=VMEM,
        compiler_params=pltpu.CompilerParams(vmem_limit_bytes=24 << 20),
    )(place, halves)


def three(x):
    top = x.astype(jnp.bfloat16)
    rest = x - top.astype(jnp.float32)
    middle = rest.astype(jnp.bfloat16)
    bottom = (rest - middle.astype(jnp.float32)).astype(jnp.bfloat16)
    return top, middle, bottom


def times(x, right):
    n = x.shape[0]
    parts = three(x)
    total = 0.0
    for at, ref in reversed(list(enumerate(right))):
        product = lax.dot_general(
            jnp.concatenate(parts[: 3 - at], 0),
            ref[...],
            NN,
            preferred_element_type=jnp.float32,
        )
        for k in reversed(range(3 - at)):
            total = total + product[k * n : (k + 1) * n]
    return total


def triangle(strips_ref):
    zero = jnp.zeros((BLOCK, BLOCK), jnp.float32)
    strip = {}
    for at, ((i, j), other) in enumerate(STRIPS[1:], 1):
        strip[i, j // 2] = strips_ref[at]
    ends = strips_ref[0]
    strip[0, 0] = jnp.concatenate([ends[:, :BLOCK], strip[1, 0][:, :BLOCK].T], 1)
    strip[8, 4] = jnp.concatenate([ends[:, BLOCK:], zero], 1)
    blank = jnp.concatenate([zero, zero], 1)
    return {
        (i, j): jnp.concatenate([strip[2 * i, j], strip.get((2 * i + 1, j), blank)], 0)
        for i, j in PAIRS
    }


def chain_kernel(place_ref, strips_ref, halves_ref, out_ref, g0, g1, t0, t1, t2):
    first_row = place_ref[2]
    blocks = triangle(strips_ref)
    row = lax.broadcasted_iota(jnp.int32, (TILE, TILE), 0)
    column = lax.broadcasted_iota(jnp.int32, (TILE, TILE), 1)
    diagonal = jnp.zeros((TILE, TILE), jnp.float32)
    for i in range(5):
        diagonal += jnp.where(row == column, blocks[i, i], 0.0)
    squares = jnp.sum(jnp.sum(diagonal, axis=0, keepdims=True), axis=1, keepdims=True)
    scale = GAIN / (GAIN * jnp.sqrt(squares) + 1e-07)
    for i, j in PAIRS:
        block = (blocks[i, j] * scale) * scale
        here = (slice(i * TILE, (i + 1) * TILE), slice(j * TILE, (j + 1) * TILE))
        for ref, part in zip((g0, g1), three(block)):
            ref[here] = part
        if i != j:
            for ref, part in zip((g0, g1), three(block.T)):
                ref[here[1], here[0]] = part
    for half in range(2):
        for ref, part in zip((t0, t1, t2), three(halves_ref[half])):
            ref[:KV_ROWS, half * TILE : (half + 1) * TILE] = part
    for ref in (t0, t1, t2):
        ref[KV_ROWS:, :] = jnp.zeros((PADDED - KV_ROWS, 2 * TILE), jnp.bfloat16)
    g, t = (g0, g1), (t0, t1, t2)

    r = lax.broadcasted_iota(jnp.int32, (32, PADDED), 0)
    k = lax.broadcasted_iota(jnp.int32, (32, PADDED), 1)
    wanted = first_row + 144 * (r >> 3) + (r & 7)
    pick = jnp.where(jnp.logical_and(k == wanted, (r & 7) < 6), 1.0, 0.0)

    def poly(x):
        once = times(x, g)
        return coef_a * x + coef_b * once + coef_c * times(once, g)

    first = poly(pick)
    second = times(poly(poly(first)), g)
    third = times(poly(poly(second)), g)
    rows = coef_a * first + coef_b * second + coef_c * third
    gain = (0.2 * math.sqrt(max(KV_ROWS, D))) * scale
    both = times(jnp.concatenate([rows, pick], 0), t)
    update, own = gain * both[:32], both[32:]
    for x in range(4):
        out_ref[x, :8, :] = update[8 * x : 8 * x + 8]
        out_ref[x, 8:, :] = own[8 * x : 8 * x + 8]


def chain(place, strips, halves):
    return pl.pallas_call(
        chain_kernel,
        out_shape=jax.ShapeDtypeStruct((4, 16, 2 * TILE), jnp.float32),
        in_specs=[SMEM, VMEM, VMEM],
        out_specs=VMEM,
        scratch_shapes=[pltpu.VMEM((PADDED, PADDED), jnp.bfloat16)] * 2
        + [pltpu.VMEM((PADDED, 2 * TILE), jnp.bfloat16)] * 3,
        compiler_params=pltpu.CompilerParams(vmem_limit_bytes=24 << 20),
    )(place, strips, halves)


def finish_kernel(got_ref, momentum_ref, update_ref, new_ref, update_half, sum_half):
    for half in range(2):
        columns = slice(half * TILE, (half + 1) * TILE)
        for m in range(MATS):
            rows = pl.ds(m, 6, stride=MATS)
            update_half[rows, :] = got_ref[m, 0:6, columns]
            sum_half[rows, :] = got_ref[m, 8:14, columns]
        momentum = momentum_ref[:, columns]
        update_ref[:, columns] = update_half[...]
        new_ref[:, columns] = 0.95 * momentum + (sum_half[...] - KAPPA * momentum)


def finish(got, momentum):
    shape = jax.ShapeDtypeStruct(momentum.shape, jnp.float32)
    return pl.pallas_call(
        finish_kernel,
        out_shape=(shape, shape),
        in_specs=[VMEM, VMEM],
        out_specs=(VMEM, VMEM),
        scratch_shapes=[pltpu.VMEM((24, TILE), jnp.float32)] * 2,
        compiler_params=pltpu.CompilerParams(vmem_limit_bytes=4 << 20),
    )(got, momentum)


def exchange(x, axis):
    return lax.all_to_all(x, axis, split_axis=0, concat_axis=0, tiled=True)


def spread(x, axis, count):
    return exchange(jnp.broadcast_to(x[None], (count, *x.shape)), axis)


def per_device(partials, momentum):
    w, v, x, c = (lax.axis_index(name) for name in ("w", "v", "x", "c"))
    z = 3 * w + v
    first_row = 48 * v + 12 * x + 6 * c
    strip = c * 12 + v * 4 + x
    place = jnp.stack([c, (z * 4 + x) * 2 + c, first_row, strip]).astype(jnp.int32)
    send = to_send(place, partials[0], momentum)
    got = lax.ppermute(send, "c", [(0, 1), (1, 0)])
    keep = to_keep(place, partials[0], momentum)
    near = jnp.sum(exchange(keep + got, ("v", "x")), axis=0)
    own = jnp.sum(exchange(near, "w"), axis=0)
    half = spread(own, ("v", "x"), 12).reshape(KV_ROWS, TILE)
    halves = lax.all_gather(half, "c", axis=0, tiled=False)
    mine = jnp.sum(spread(gram(place, halves), "y", 8), axis=0)
    strips = lax.all_gather(spread(mine, ("v", "x"), 12), "c", axis=0, tiled=True)
    done = chain(place, strips, halves)
    return finish(exchange(done, "w"), momentum)


def solution(mesh):
    fine = Mesh(mesh.devices.reshape(4, 3, 4, 2, 8), ("w", "v", "x", "c", "y"))
    rows = ("w", "v", "x", "c")
    return jax.shard_map(
        per_device,
        mesh=fine,
        in_specs=(P(rows, None, "y"), P(rows, "y")),
        out_specs=(P(rows, "y"), P(rows, "y")),
        check_vma=False,
    )
```

```python
import functools
import math

import jax
import jax.numpy as jnp
import numpy as np
from jax import lax
from jax.experimental import pallas as pl
from jax.experimental.pallas import tpu as pltpu
from jax.sharding import Mesh
from jax.sharding import PartitionSpec as P

D = 2048
KV_ROWS = 576
MATS = 4
PADDED = 640
TILE = 128

coef_a = 3.4445
coef_b = -4.775
coef_c = 2.0315

GAIN = 1.95
KAPPA = 0.9025 / 1.95

BLOCK = 64

STRIPS = [((0, 0), (8, 8))]
STRIPS += [
    ((i, 2 * j), (i, 2 * j + 1))
    for i in range(1, 9)
    for j in range(i // 2 + 1)
    if (i, j) != (8, 4)
]
STARTS = [next(n for n, (a, _) in enumerate(STRIPS) if a[0] == i) for i in range(9)]
PAIRS = [(i, j) for i in range(5) for j in range(i + 1)]

CHUNKS = 4
SEND_LIMIT = 54788096

VMEM = pl.BlockSpec(memory_space=pltpu.VMEM)
HBM = pl.BlockSpec(memory_space=pltpu.HBM)
NT = (((1,), (1,)), ((), ()))
NN = (((1,), (0,)), ((), ()))


def place():
    w, v, x, c = (lax.axis_index(name) for name in ("w", "v", "x", "c"))
    first = (((3 * w + v) * 4 + x) * 2 + c) * 24
    return c, first, 48 * v + 12 * x + 6 * c, c * 12 + v * 4 + x


def sort_chunk(q, first, own_rows, wide, out_ref):
    chunk = wide.shape[0] // CHUNKS

    @pl.when(first // chunk == q)
    def _():
        wide[pl.ds(pl.multiple_of(first, 8), 24), :] += KAPPA * own_rows

    for m in range(MATS):
        rows = pl.ds(q * chunk + m, chunk // MATS, stride=MATS)
        groups = slice(q * 12 // CHUNKS, (q + 1) * 12 // CHUNKS)
        out_ref[groups, m] = wide[rows, :].reshape(-1, 48, TILE)


def send_kernel(partial_ref, held, out_ref, raw, wide, sems):
    core, first = place()[:2]
    chunk = raw.shape[0] // CHUNKS
    columns = pl.ds(pl.multiple_of((1 - core) * TILE, TILE), TILE)
    copies = []
    for q in range(CHUNKS):
        rows = pl.ds(q * chunk, chunk)
        copies.append(
            pltpu.make_async_copy(partial_ref.at[rows, columns], raw.at[rows], sems.at[q])
        )
    for copy in copies:
        copy.start()
    own_rows = held[:, columns]
    for q in range(CHUNKS):
        copies[q].wait()
        rows = slice(q * chunk, (q + 1) * chunk)
        wide[rows, :] = raw[rows, :].astype(jnp.float32)
        sort_chunk(q, first, own_rows, wide, out_ref)


def keep_kernel(raw, held, out_ref, wide):
    core, first = place()[:2]
    chunk = raw.shape[0] // CHUNKS
    columns = pl.ds(pl.multiple_of(core * TILE, TILE), TILE)
    own_rows = held[:, columns]
    for q in range(CHUNKS):
        rows = slice(q * chunk, (q + 1) * chunk)
        wide[rows, :] = raw[rows, columns].astype(jnp.float32)
        sort_chunk(q, first, own_rows, wide, out_ref)


HALF = jax.ShapeDtypeStruct((12, MATS, 48, TILE), jnp.float32)
WIDE = pltpu.VMEM((MATS * KV_ROWS, TILE), jnp.float32)
COST = pl.CostEstimate(flops=1 << 20, bytes_accessed=3 << 20, transcendentals=0)


def to_send(partial, momentum):
    return pl.pallas_call(
        send_kernel,
        out_shape=HALF,
        in_specs=[HBM, VMEM],
        out_specs=VMEM,
        scratch_shapes=[
            pltpu.VMEM((MATS * KV_ROWS, TILE), jnp.bfloat16),
            WIDE,
            pltpu.SemaphoreType.DMA((CHUNKS,)),
        ],
        compiler_params=pltpu.CompilerParams(vmem_limit_bytes=SEND_LIMIT),
        cost_estimate=COST,
    )(partial, momentum)


def to_keep(partial, momentum):
    return pl.pallas_call(
        keep_kernel,
        out_shape=HALF,
        in_specs=[VMEM, VMEM],
        out_specs=VMEM,
        scratch_shapes=[WIDE],
        compiler_params=pltpu.CompilerParams(vmem_limit_bytes=16 << 20),
        cost_estimate=COST,
    )(partial, momentum)


def gram_kernel(halves_ref, out_ref):
    strip = place()[3]
    i, start = jnp.int32(0), jnp.int32(0)
    for begin, step in zip(STARTS[1:], np.diff(STARTS)):
        past = strip >= begin
        i += past.astype(jnp.int32)
        start += jnp.where(past, int(step), 0)
    j = 2 * (strip - start)
    ends = strip == 0
    sides = [(i, j), (jnp.where(ends, 8, i), jnp.where(ends, 8, j + 1))]
    for side, pair in enumerate(sides):
        picks = [pl.ds(pl.multiple_of(k * BLOCK, BLOCK), BLOCK) for k in pair]
        left, right = (
            jnp.concatenate([halves_ref[0, rows, :], halves_ref[1, rows, :]], 1) for rows in picks
        )
        out_ref[:, side * BLOCK : (side + 1) * BLOCK] = lax.dot_general(
            left,
            right,
            NT,
            precision=lax.Precision.HIGHEST,
            preferred_element_type=jnp.float32,
        )


def gram(halves):
    return pl.pallas_call(
        gram_kernel,
        out_shape=jax.ShapeDtypeStruct((BLOCK, TILE), jnp.float32),
        in_specs=[VMEM],
        out_specs=VMEM,
        compiler_params=pltpu.CompilerParams(vmem_limit_bytes=24 << 20),
    )(halves)


def three(x):
    top = x.astype(jnp.bfloat16)
    rest = x - top.astype(jnp.float32)
    middle = rest.astype(jnp.bfloat16)
    bottom = (rest - middle.astype(jnp.float32)).astype(jnp.bfloat16)
    return top, middle, bottom


def times(x, right):
    n = x.shape[0]
    parts = three(x)
    total = 0.0
    for at, ref in reversed(list(enumerate(right))):
        product = lax.dot_general(
            jnp.concatenate(parts[: 3 - at], 0),
            ref[...],
            NN,
            preferred_element_type=jnp.float32,
        )
        for k in reversed(range(3 - at)):
            total = total + product[k * n : (k + 1) * n]
    return total


def triangle(strips_ref):
    zero = jnp.zeros((BLOCK, BLOCK), jnp.float32)
    strip = {}
    for at, ((i, j), other) in enumerate(STRIPS[1:], 1):
        strip[i, j // 2] = strips_ref[at]
    ends = strips_ref[0]
    strip[0, 0] = jnp.concatenate([ends[:, :BLOCK], strip[1, 0][:, :BLOCK].T], 1)
    strip[8, 4] = jnp.concatenate([ends[:, BLOCK:], zero], 1)
    blank = jnp.concatenate([zero, zero], 1)
    return {
        (i, j): jnp.concatenate([strip[2 * i, j], strip.get((2 * i + 1, j), blank)], 0)
        for i, j in PAIRS
    }


def chain_kernel(strips_ref, halves_ref, out_ref, g0, g1, t0, t1, t2):
    first_row = place()[2]
    blocks = triangle(strips_ref)
    row = lax.broadcasted_iota(jnp.int32, (TILE, TILE), 0)
    column = lax.broadcasted_iota(jnp.int32, (TILE, TILE), 1)
    diagonal = jnp.zeros((TILE, TILE), jnp.float32)
    for i in range(5):
        diagonal += jnp.where(row == column, blocks[i, i], 0.0)
    squares = jnp.sum(jnp.sum(diagonal, axis=0, keepdims=True), axis=1, keepdims=True)
    scale = GAIN / (GAIN * jnp.sqrt(squares) + 1e-07)
    for i, j in PAIRS:
        block = (blocks[i, j] * scale) * scale
        here = (slice(i * TILE, (i + 1) * TILE), slice(j * TILE, (j + 1) * TILE))
        for ref, part in zip((g0, g1), three(block)):
            ref[here] = part
        if i != j:
            for ref, part in zip((g0, g1), three(block.T)):
                ref[here[1], here[0]] = part
    for half in range(2):
        for ref, part in zip((t0, t1, t2), three(halves_ref[half])):
            ref[:KV_ROWS, half * TILE : (half + 1) * TILE] = part
    for ref in (t0, t1, t2):
        ref[KV_ROWS:, :] = jnp.zeros((PADDED - KV_ROWS, 2 * TILE), jnp.bfloat16)
    g, t = (g0, g1), (t0, t1, t2)

    r = lax.broadcasted_iota(jnp.int32, (32, PADDED), 0)
    k = lax.broadcasted_iota(jnp.int32, (32, PADDED), 1)
    wanted = first_row + 144 * (r >> 3) + (r & 7)
    pick = jnp.where(jnp.logical_and(k == wanted, (r & 7) < 6), 1.0, 0.0)

    def poly(x):
        once = times(x, g)
        return coef_a * x + coef_b * once + coef_c * times(once, g)

    first = poly(pick)
    second = times(poly(poly(first)), g)
    third = times(poly(poly(second)), g)
    rows = coef_a * first + coef_b * second + coef_c * third
    gain = (0.2 * math.sqrt(max(KV_ROWS, D))) * scale
    both = times(jnp.concatenate([rows, pick], 0), t)
    update, own = gain * both[:32], both[32:]
    for x in range(4):
        out_ref[x, :8, :] = update[8 * x : 8 * x + 8]
        out_ref[x, 8:, :] = own[8 * x : 8 * x + 8]


def chain(strips, halves):
    return pl.pallas_call(
        chain_kernel,
        out_shape=jax.ShapeDtypeStruct((4, 16, 2 * TILE), jnp.float32),
        in_specs=[VMEM, VMEM],
        out_specs=VMEM,
        scratch_shapes=[pltpu.VMEM((PADDED, PADDED), jnp.bfloat16)] * 2
        + [pltpu.VMEM((PADDED, 2 * TILE), jnp.bfloat16)] * 3,
        compiler_params=pltpu.CompilerParams(vmem_limit_bytes=24 << 20),
    )(strips, halves)


def finish_kernel(got_ref, momentum_ref, update_ref, new_ref, update_half, sum_half):
    for half in range(2):
        columns = slice(half * TILE, (half + 1) * TILE)
        for m in range(MATS):
            rows = pl.ds(m, 6, stride=MATS)
            update_half[rows, :] = got_ref[m, 0:6, columns]
            sum_half[rows, :] = got_ref[m, 8:14, columns]
        momentum = momentum_ref[:, columns]
        update_ref[:, columns] = update_half[...]
        new_ref[:, columns] = 0.95 * momentum + (sum_half[...] - KAPPA * momentum)


def finish(got, momentum):
    shape = jax.ShapeDtypeStruct(momentum.shape, jnp.float32)
    return pl.pallas_call(
        finish_kernel,
        out_shape=(shape, shape),
        in_specs=[VMEM, VMEM],
        out_specs=(VMEM, VMEM),
        scratch_shapes=[pltpu.VMEM((24, TILE), jnp.float32)] * 2,
        compiler_params=pltpu.CompilerParams(vmem_limit_bytes=4 << 20),
    )(got, momentum)


def exchange(x, axis):
    return lax.all_to_all(x, axis, split_axis=0, concat_axis=0, tiled=True)


def spread(x, axis, count):
    return exchange(jnp.broadcast_to(x[None], (count, *x.shape)), axis)


def per_device(partials, momentum):
    send = to_send(partials[0], momentum)
    got = lax.ppermute(send, "c", [(0, 1), (1, 0)])
    keep = to_keep(partials[0], momentum)
    near = jnp.sum(exchange(keep + got, ("v", "x")), axis=0)
    own = jnp.sum(exchange(near, "w"), axis=0)
    half = spread(own, ("v", "x"), 12).reshape(KV_ROWS, TILE)
    halves = lax.all_gather(half, "c", axis=0, tiled=False)
    mine = jnp.sum(spread(gram(halves), "y", 8), axis=0)
    strips = lax.all_gather(spread(mine, ("v", "x"), 12), "c", axis=0, tiled=True)
    done = chain(strips, halves)
    return finish(exchange(done, "w"), momentum)


def solution(mesh):
    fine = Mesh(mesh.devices.reshape(4, 3, 4, 2, 8), ("w", "v", "x", "c", "y"))
    rows = ("w", "v", "x", "c")
    return jax.shard_map(
        per_device,
        mesh=fine,
        in_specs=(P(rows, None, "y"), P(rows, "y")),
        out_specs=(P(rows, "y"), P(rows, "y")),
        check_vma=False,
    )
```

```python
import functools
import math

import jax
import jax.numpy as jnp
import numpy as np
from jax import lax
from jax.experimental import pallas as pl
from jax.experimental.pallas import tpu as pltpu
from jax.sharding import Mesh
from jax.sharding import PartitionSpec as P

D = 2048
KV_ROWS = 576
MATS = 4
PADDED = 640
TILE = 128

coef_a = 3.4445
coef_b = -4.775
coef_c = 2.0315

GAIN = 1.95
KAPPA = 0.9025 / 1.95

BLOCK = 64

STRIPS = [((0, 0), (8, 8))]
STRIPS += [
    ((i, 2 * j), (i, 2 * j + 1))
    for i in range(1, 9)
    for j in range(i // 2 + 1)
    if (i, j) != (8, 4)
]
STARTS = [next(n for n, (a, _) in enumerate(STRIPS) if a[0] == i) for i in range(9)]
PAIRS = [(i, j) for i in range(5) for j in range(i + 1)]

CHUNKS = 4
SEND_LIMIT = 54788096

VMEM = pl.BlockSpec(memory_space=pltpu.VMEM)
HBM = pl.BlockSpec(memory_space=pltpu.HBM)
NT = (((1,), (1,)), ((), ()))
NN = (((1,), (0,)), ((), ()))


def place():
    w, v, x, c = (lax.axis_index(name) for name in ("w", "v", "x", "c"))
    first = (((3 * w + v) * 4 + x) * 2 + c) * 24
    return c, first, 48 * v + 12 * x + 6 * c, c * 12 + v * 4 + x


def sort_chunk(q, first, own_rows, wide, out_ref):
    chunk = wide.shape[0] // CHUNKS

    if own_rows is not None:

        @pl.when(first // chunk == q)
        def _():
            wide[pl.ds(pl.multiple_of(first, 8), 24), :] += KAPPA * own_rows

    for m in range(MATS):
        rows = pl.ds(q * chunk + m, chunk // MATS, stride=MATS)
        groups = slice(q * 12 // CHUNKS, (q + 1) * 12 // CHUNKS)
        out_ref[groups, m] = wide[rows, :].reshape(-1, 48, TILE)


def send_kernel(partial_ref, out_ref, raw, wide, sems):
    core, first = place()[:2]
    chunk = raw.shape[0] // CHUNKS
    columns = pl.ds(pl.multiple_of((1 - core) * TILE, TILE), TILE)
    copies = []
    for q in range(CHUNKS):
        rows = pl.ds(q * chunk, chunk)
        copies.append(
            pltpu.make_async_copy(partial_ref.at[rows, columns], raw.at[rows], sems.at[q])
        )
    for copy in copies:
        copy.start()
    for q in range(CHUNKS):
        copies[q].wait()
        rows = slice(q * chunk, (q + 1) * chunk)
        wide[rows, :] = raw[rows, :].astype(jnp.float32)
        sort_chunk(q, first, None, wide, out_ref)


def momentum_kernel(held, half_ref, out_ref):
    core, first = place()[:2]
    own = first // MATS
    group, start = own // 48, own % 48
    rows = KAPPA * held[:, pl.ds(pl.multiple_of((1 - core) * TILE, TILE), TILE)]
    at = lax.broadcasted_iota(jnp.int32, (48, TILE), 0) - start
    out_ref[...] = half_ref[...]
    for m in range(MATS):
        total = jnp.zeros((48, TILE), jnp.float32)
        for j in range(6):
            total = jnp.where(at == j, rows[MATS * j + m : MATS * j + m + 1, :], total)
        out_ref[group, m] += total


def keep_kernel(raw, held, out_ref, wide):
    core, first = place()[:2]
    chunk = raw.shape[0] // CHUNKS
    columns = pl.ds(pl.multiple_of(core * TILE, TILE), TILE)
    own_rows = held[:, columns]
    for q in range(CHUNKS):
        rows = slice(q * chunk, (q + 1) * chunk)
        wide[rows, :] = raw[rows, columns].astype(jnp.float32)
        sort_chunk(q, first, own_rows, wide, out_ref)


HALF = jax.ShapeDtypeStruct((12, MATS, 48, TILE), jnp.float32)
WIDE = pltpu.VMEM((MATS * KV_ROWS, TILE), jnp.float32)
COST = pl.CostEstimate(flops=1 << 20, bytes_accessed=3 << 20, transcendentals=0)


def to_send(partial, momentum):
    half = pl.pallas_call(
        send_kernel,
        out_shape=HALF,
        in_specs=[HBM],
        out_specs=VMEM,
        scratch_shapes=[
            pltpu.VMEM((MATS * KV_ROWS, TILE), jnp.bfloat16),
            WIDE,
            pltpu.SemaphoreType.DMA((CHUNKS,)),
        ],
        compiler_params=pltpu.CompilerParams(vmem_limit_bytes=SEND_LIMIT),
        cost_estimate=COST,
    )(partial)
    return pl.pallas_call(
        momentum_kernel,
        out_shape=HALF,
        in_specs=[VMEM, VMEM],
        out_specs=VMEM,
        compiler_params=pltpu.CompilerParams(vmem_limit_bytes=8 << 20),
    )(momentum, half)


def to_keep(partial, momentum):
    return pl.pallas_call(
        keep_kernel,
        out_shape=HALF,
        in_specs=[VMEM, VMEM],
        out_specs=VMEM,
        scratch_shapes=[WIDE],
        compiler_params=pltpu.CompilerParams(vmem_limit_bytes=16 << 20),
        cost_estimate=COST,
    )(partial, momentum)


def gram_kernel(halves_ref, out_ref):
    strip = place()[3]
    i, start = jnp.int32(0), jnp.int32(0)
    for begin, step in zip(STARTS[1:], np.diff(STARTS)):
        past = strip >= begin
        i += past.astype(jnp.int32)
        start += jnp.where(past, int(step), 0)
    j = 2 * (strip - start)
    ends = strip == 0
    sides = [(i, j), (jnp.where(ends, 8, i), jnp.where(ends, 8, j + 1))]
    for side, pair in enumerate(sides):
        picks = [pl.ds(pl.multiple_of(k * BLOCK, BLOCK), BLOCK) for k in pair]
        left, right = (
            jnp.concatenate([halves_ref[0, rows, :], halves_ref[1, rows, :]], 1) for rows in picks
        )
        out_ref[:, side * BLOCK : (side + 1) * BLOCK] = lax.dot_general(
            left,
            right,
            NT,
            precision=lax.Precision.HIGHEST,
            preferred_element_type=jnp.float32,
        )


def gram(halves):
    return pl.pallas_call(
        gram_kernel,
        out_shape=jax.ShapeDtypeStruct((BLOCK, TILE), jnp.float32),
        in_specs=[VMEM],
        out_specs=VMEM,
        compiler_params=pltpu.CompilerParams(vmem_limit_bytes=24 << 20),
    )(halves)


def three(x):
    top = x.astype(jnp.bfloat16)
    rest = x - top.astype(jnp.float32)
    middle = rest.astype(jnp.bfloat16)
    bottom = (rest - middle.astype(jnp.float32)).astype(jnp.bfloat16)
    return top, middle, bottom


def times(x, right):
    n = x.shape[0]
    parts = three(x)
    total = 0.0
    for at, ref in reversed(list(enumerate(right))):
        product = lax.dot_general(
            jnp.concatenate(parts[: 3 - at], 0),
            ref[...],
            NN,
            preferred_element_type=jnp.float32,
        )
        for k in reversed(range(3 - at)):
            total = total + product[k * n : (k + 1) * n]
    return total


def triangle(strips_ref):
    zero = jnp.zeros((BLOCK, BLOCK), jnp.float32)
    strip = {}
    for at, ((i, j), other) in enumerate(STRIPS[1:], 1):
        strip[i, j // 2] = strips_ref[at]
    ends = strips_ref[0]
    strip[0, 0] = jnp.concatenate([ends[:, :BLOCK], strip[1, 0][:, :BLOCK].T], 1)
    strip[8, 4] = jnp.concatenate([ends[:, BLOCK:], zero], 1)
    blank = jnp.concatenate([zero, zero], 1)
    return {
        (i, j): jnp.concatenate([strip[2 * i, j], strip.get((2 * i + 1, j), blank)], 0)
        for i, j in PAIRS
    }


def chain_kernel(strips_ref, halves_ref, out_ref, g0, g1, t0, t1, t2):
    first_row = place()[2]
    blocks = triangle(strips_ref)
    row = lax.broadcasted_iota(jnp.int32, (TILE, TILE), 0)
    column = lax.broadcasted_iota(jnp.int32, (TILE, TILE), 1)
    diagonal = jnp.zeros((TILE, TILE), jnp.float32)
    for i in range(5):
        diagonal += jnp.where(row == column, blocks[i, i], 0.0)
    squares = jnp.sum(jnp.sum(diagonal, axis=0, keepdims=True), axis=1, keepdims=True)
    scale = GAIN / (GAIN * jnp.sqrt(squares) + 1e-07)
    for i, j in PAIRS:
        block = (blocks[i, j] * scale) * scale
        here = (slice(i * TILE, (i + 1) * TILE), slice(j * TILE, (j + 1) * TILE))
        for ref, part in zip((g0, g1), three(block)):
            ref[here] = part
        if i != j:
            for ref, part in zip((g0, g1), three(block.T)):
                ref[here[1], here[0]] = part
    for half in range(2):
        for ref, part in zip((t0, t1, t2), three(halves_ref[half])):
            ref[:KV_ROWS, half * TILE : (half + 1) * TILE] = part
    for ref in (t0, t1, t2):
        ref[KV_ROWS:, :] = jnp.zeros((PADDED - KV_ROWS, 2 * TILE), jnp.bfloat16)
    g, t = (g0, g1), (t0, t1, t2)

    r = lax.broadcasted_iota(jnp.int32, (32, PADDED), 0)
    k = lax.broadcasted_iota(jnp.int32, (32, PADDED), 1)
    wanted = first_row + 144 * (r >> 3) + (r & 7)
    pick = jnp.where(jnp.logical_and(k == wanted, (r & 7) < 6), 1.0, 0.0)

    def poly(x):
        once = times(x, g)
        return coef_a * x + coef_b * once + coef_c * times(once, g)

    first = poly(pick)
    second = times(poly(poly(first)), g)
    third = times(poly(poly(second)), g)
    rows = coef_a * first + coef_b * second + coef_c * third
    gain = (0.2 * math.sqrt(max(KV_ROWS, D))) * scale
    both = times(jnp.concatenate([rows, pick], 0), t)
    update, own = gain * both[:32], both[32:]
    for x in range(4):
        out_ref[x, :8, :] = update[8 * x : 8 * x + 8]
        out_ref[x, 8:, :] = own[8 * x : 8 * x + 8]


def chain(strips, halves):
    return pl.pallas_call(
        chain_kernel,
        out_shape=jax.ShapeDtypeStruct((4, 16, 2 * TILE), jnp.float32),
        in_specs=[VMEM, VMEM],
        out_specs=VMEM,
        scratch_shapes=[pltpu.VMEM((PADDED, PADDED), jnp.bfloat16)] * 2
        + [pltpu.VMEM((PADDED, 2 * TILE), jnp.bfloat16)] * 3,
        compiler_params=pltpu.CompilerParams(vmem_limit_bytes=24 << 20),
    )(strips, halves)


def finish_kernel(got_ref, momentum_ref, update_ref, new_ref, update_half, sum_half):
    for half in range(2):
        columns = slice(half * TILE, (half + 1) * TILE)
        for m in range(MATS):
            rows = pl.ds(m, 6, stride=MATS)
            update_half[rows, :] = got_ref[m, 0:6, columns]
            sum_half[rows, :] = got_ref[m, 8:14, columns]
        momentum = momentum_ref[:, columns]
        update_ref[:, columns] = update_half[...]
        new_ref[:, columns] = 0.95 * momentum + (sum_half[...] - KAPPA * momentum)


def finish(got, momentum):
    shape = jax.ShapeDtypeStruct(momentum.shape, jnp.float32)
    return pl.pallas_call(
        finish_kernel,
        out_shape=(shape, shape),
        in_specs=[VMEM, VMEM],
        out_specs=(VMEM, VMEM),
        scratch_shapes=[pltpu.VMEM((24, TILE), jnp.float32)] * 2,
        compiler_params=pltpu.CompilerParams(vmem_limit_bytes=4 << 20),
    )(got, momentum)


def exchange(x, axis):
    return lax.all_to_all(x, axis, split_axis=0, concat_axis=0, tiled=True)


def spread(x, axis, count):
    return exchange(jnp.broadcast_to(x[None], (count, *x.shape)), axis)


def per_device(partials, momentum):
    send = to_send(partials[0], momentum)
    got = lax.ppermute(send, "c", [(0, 1), (1, 0)])
    keep = to_keep(partials[0], momentum)
    near = jnp.sum(exchange(keep + got, ("v", "x")), axis=0)
    own = jnp.sum(exchange(near, "w"), axis=0)
    half = spread(own, ("v", "x"), 12).reshape(KV_ROWS, TILE)
    halves = lax.all_gather(half, "c", axis=0, tiled=False)
    mine = jnp.sum(spread(gram(halves), "y", 8), axis=0)
    strips = lax.all_gather(spread(mine, ("v", "x"), 12), "c", axis=0, tiled=True)
    done = chain(strips, halves)
    return finish(exchange(done, "w"), momentum)


def solution(mesh):
    fine = Mesh(mesh.devices.reshape(4, 3, 4, 2, 8), ("w", "v", "x", "c", "y"))
    rows = ("w", "v", "x", "c")
    return jax.shard_map(
        per_device,
        mesh=fine,
        in_specs=(P(rows, None, "y"), P(rows, "y")),
        out_specs=(P(rows, "y"), P(rows, "y")),
        check_vma=False,
    )
```
